32 devices in a mesh: shards: 2 (over x), context: 4 (over y, core), tensor: 4 (over z).
Axes of the slice: x: 2, y: 2, z: 4, core: 2. Of those that a mesh axis runs over, the one named last changes fastest.
Arguments:
- hidden_in: bfloat16 [2, 1024, 1024], P('shards', 'context'), may hold values from -6 to 6
- positions: int32 [2, 1024], P('shards'), may hold values from 0 to 1023, each once within a row
- routes: int32 [2, 1024, 8], P('shards', 'context'), may hold values from 0 to 31, all different within a row; in each aligned block of 256 rows (0 to 255, 256 to 511, ..., all dimensions but the last counted through in order) at most 96 rows name the same one
- out_grad: bfloat16 [2, 1024, 1024], P('shards', 'context'), may hold values from -6 to 6
- attn_gain: bfloat16 [1024], P(('shards', 'context')), may hold values from 0.5 to 1.5
- query_weight: bfloat16 [1024, 1024], P(('shards', 'context'), 'tensor'), may hold values from -0.75 to 0.75
- key_matrix: bfloat16 [1024, 512], P(('shards', 'context'), 'tensor'), may hold values from -0.75 to 0.75
- value_matrix: bfloat16 [1024, 512], P(('shards', 'context'), 'tensor'), may hold values from -0.1875 to 0.1875
- out_weight: bfloat16 [1024, 1024], P(('shards', 'context'), 'tensor'), may hold values from -3 to 3
- moe_gain: bfloat16 [1024], P(('shards', 'context')), may hold values from 0.5 to 1.5
- router_weight: bfloat16 [1024, 32], P(('shards', 'context')), may hold values from -0.09375 to 0.09375
- gate_weight: bfloat16 [32, 1024, 512], P('context', 'shards', 'tensor'), may hold values from -0.1875 to 0.1875
- up_weight: bfloat16 [32, 1024, 512], P('context', 'shards', 'tensor'), may hold values from -0.1875 to 0.1875
- down_weight: bfloat16 [32, 1024, 512], P('context', 'shards', 'tensor'), may hold values from -6 to 6
Outputs:
- block_out: bfloat16 [2, 1024, 1024], P('shards', 'context')
- in_grad: float32 [2, 1024, 1024], P('shards', 'context')
- attn_gain_grad: float32 [1024], P(('shards', 'context'))
- query_weight_grad: float32 [1024, 1024], P(('shards', 'context'), 'tensor')
- key_weight_grad: float32 [1024, 512], P(('shards', 'context'), 'tensor')
- value_weight_grad: float32 [1024, 512], P(('shards', 'context'), 'tensor')
- out_weight_grad: float32 [1024, 1024], P(('shards', 'context'), 'tensor')
- moe_gain_grad: float32 [1024], P(('shards', 'context'))
- router_grad: float32 [1024, 32], P(('shards', 'context'))
- gate_weight_grad: float32 [32, 1024, 512], P('context', 'shards', 'tensor')
- up_weight_grad: float32 [32, 1024, 512], P('context', 'shards', 'tensor')
- down_weight_grad: float32 [32, 1024, 512], P('context', 'shards', 'tensor')
The draws below stay inside these ranges and needn't reach their ends.
Inputs may be any that keep to these rules, and one draw needn't show every extreme that they name: `positions`: each sequence's row holds every position once. `routes`: each token names 8 different experts; among the tokens of one device (aligned blocks of 256 tokens) no expert is named more than 96 times, and in every draw some block names some expert exactly 96 times.
All inputs are finite; a program needn't handle non-finite values.
Results may differ from the reference program's by a relative error of at most 0.02.
Values may be sent and summed in bfloat16 or wider, within the bound.
No kernel may reach another device: no remote copies, remote signals or barrier semaphores. Data moves between devices by JAX's collectives and lax.ppermute only.
A program may use at most 128 MiB of HBM per device.

```python
import math
import jax
import jax.numpy as jnp
import numpy as np
from jax import lax

MODEL_WIDTH = 1024
QUERY_HEADS = 16
KEY_VALUE_HEADS = 8
HEAD_SIZE = 64
FF = 512
EXPERTS = 32
TOPK = 8
SEQS = 2
SEQUENCE_TOKENS = 1024
ROWS = 256
CAP = 96
N_CONTEXT = 4
N_TENSOR = 4


def shard_levels(key, shape, split, least, top_value):
    def one(axis_at, shards_of):
        draws = jax.random.uniform(jax.random.fold_in(jax.random.fold_in(key, 6), axis_at), (shards_of,), jnp.float32, least / len(split), top_value / len(split))
        return jnp.repeat(jnp.exp(draws), shape[axis_at] // shards_of).reshape((-1,) + (1,) * (len(shape) - axis_at - 1))

    factor_of = one(*split[0])
    for cut in split[1:]:
        factor_of = factor_of * one(*cut)
    return factor_of


def assign_block(key, own, number, rows, amount, top, reach, lean):
    order = jax.random.permutation(key, amount)
    crowded, usual = shares(amount, rows * top, reach, lean, True), shares(amount, rows * top, reach, lean, False)
    places = jnp.arange(amount)

    def named(lengths, turn):
        used = int((lengths > 0).sum())
        fixed = max(1, used // 4)
        shifted = fixed + (places - fixed + turn * (used - fixed)) % max(1, amount - fixed)
        return jnp.zeros((amount,), jnp.int32).at[order[jnp.where(places < fixed, places, shifted)]].set(jnp.asarray(lengths, jnp.int32))

    lengths = jnp.where(number % 4 == 0, named(crowded, number // 4), named(usual, number - number // 4 - 1))
    mixed = jax.random.permutation(jax.random.fold_in(own, 3), amount)
    giver, taker = mixed[0:amount // 2 * 2:2], mixed[1:amount // 2 * 2:2]
    room = jnp.minimum(lengths[giver] - 1, reach - lengths[taker]) // 2
    room = jnp.where((giver == order[0]) | (taker == order[0]) | (lengths[taker] == 0), 0, jnp.maximum(room, 0))
    shifted = jax.random.randint(jax.random.fold_in(own, 4), (amount // 2,), 0, 1 << 20) % (room + 1)
    lengths = lengths.at[giver].add(-shifted).at[taker].add(shifted)
    items = jnp.searchsorted(jnp.cumsum(lengths), jnp.arange(rows * top), side="right").astype(jnp.int32)
    table = items.reshape(top, rows).T
    table = table[jax.random.permutation(jax.random.fold_in(own, 1), rows)]
    turn = jax.random.randint(jax.random.fold_in(own, 2), (rows, 1), 0, top)
    return jnp.take_along_axis(table, (jnp.arange(top)[None, :] + turn) % top, axis=1)


def shares(amount, total, limit, skew, full):
    loads = [(1 << 20) // math.isqrt(standing ** skew) + 1 for standing in range(1, amount + 1)]
    largest = limit if full else min(limit, max(-(-total // amount), total * loads[0] // sum(loads)))
    least = 1 if total - largest >= amount - 1 else 0
    counts, rest = [largest] + [least] * (amount - 1), total - largest - least * (amount - 1)
    while rest > 0:
        movable = [i for i in range(1, amount) if counts[i] < largest] or [i for i in range(1, amount) if counts[i] < limit]
        mass, left = sum([loads[i] for i in movable]), rest
        for i in movable:
            extra = min(limit - counts[i], max(1, left * loads[i] // mass), rest)
            counts[i] = counts[i] + extra
            rest = rest - extra
    return np.array(counts)


def bell_draw(rng, shape, scale, reach, shards=(), kind=jnp.bfloat16):
    values = scale * jax.random.normal(rng, shape, jnp.float32)
    if shards:
        values = values * shard_levels(rng, shape, shards, -0.22, 0.18)
    return jnp.clip(values, -reach, reach).astype(kind)


def setup_inputs(seed: int = 0) -> dict:
    keys = jax.random.split(jax.random.key(seed), 15)
    hidden_in = bell_draw(keys[0], (SEQS, SEQUENCE_TOKENS, MODEL_WIDTH), 1.0, 6.0, ((0, 2), (1, 4)))
    positions = jax.vmap(lambda own: jax.random.permutation(own, SEQUENCE_TOKENS))(jax.random.split(keys[1], SEQS)).reshape((SEQS, SEQUENCE_TOKENS)).astype(jnp.int32)
    routes_keys = jax.random.split(jax.random.fold_in(keys[2], 1), SEQS * SEQUENCE_TOKENS // ROWS)
    routes_turns = jax.random.permutation(jax.random.fold_in(keys[2], 3), SEQS * SEQUENCE_TOKENS // ROWS)
    routes = jax.vmap(lambda own, number: assign_block(jax.random.fold_in(keys[2], 2), own, number, ROWS, EXPERTS, TOPK, CAP, 2))(routes_keys, routes_turns).reshape((SEQS, SEQUENCE_TOKENS, TOPK))
    out_grad = bell_draw(keys[3], (SEQS, SEQUENCE_TOKENS, MODEL_WIDTH), 1.0, 6.0, ((0, 2), (1, 4)))
    attn_gain = jnp.clip(1.0 + 0.1 * jax.random.normal(keys[4], (MODEL_WIDTH,), jnp.float32), 0.5, 1.5).astype(jnp.bfloat16)
    query_weight = bell_draw(keys[5], (MODEL_WIDTH, QUERY_HEADS * HEAD_SIZE), 64 ** -0.5, 0.75, ((0, 8), (1, 4)))
    key_matrix = bell_draw(keys[6], (MODEL_WIDTH, KEY_VALUE_HEADS * HEAD_SIZE), 64 ** -0.5, 0.75, ((0, 8), (1, 4)))
    value_matrix = bell_draw(keys[7], (MODEL_WIDTH, KEY_VALUE_HEADS * HEAD_SIZE), MODEL_WIDTH ** -0.5, 0.1875, ((0, 8), (1, 4)))
    out_weight = bell_draw(keys[8], (MODEL_WIDTH, QUERY_HEADS * HEAD_SIZE), 0.5, 3.0, ((0, 8), (1, 4)))
    moe_gain = jnp.clip(1.0 + 0.1 * jax.random.normal(keys[9], (MODEL_WIDTH,), jnp.float32), 0.5, 1.5).astype(jnp.bfloat16)
    router_weight = bell_draw(keys[10], (MODEL_WIDTH, EXPERTS), (4 * MODEL_WIDTH) ** -0.5, 0.09375, ((0, 8),))
    gate_weight = bell_draw(keys[11], (EXPERTS, MODEL_WIDTH, FF), MODEL_WIDTH ** -0.5, 0.1875, ((0, 4), (1, 2), (2, 4)))
    up_weight = bell_draw(keys[12], (EXPERTS, MODEL_WIDTH, FF), MODEL_WIDTH ** -0.5, 0.1875, ((0, 4), (1, 2), (2, 4)))
    down_weight = bell_draw(keys[13], (EXPERTS, MODEL_WIDTH, FF), 1.0, 6.0, ((0, 4), (1, 2), (2, 4)))
    return dict(hidden_in=hidden_in, positions=positions, routes=routes, out_grad=out_grad, attn_gain=attn_gain, query_weight=query_weight, key_matrix=key_matrix, value_matrix=value_matrix, out_weight=out_weight, moe_gain=moe_gain, router_weight=router_weight, gate_weight=gate_weight, up_weight=up_weight, down_weight=down_weight)


NORM_EPS = 1e-06
ATTN_MULT = 0.015625
RESID_MULT = 0.22
ROPE_BASE = 10000.0
HIGHEST = lax.Precision.HIGHEST

@jax.custom_vjp
def lower_part(v):
    return lax.optimization_barrier(v.astype(jnp.bfloat16)).astype(jnp.float32)

@jax.custom_vjp
def low_back(v):
    return v

def low_keep(v):
    return (lower_part(v), None)

def low_pass(kept, grad):
    return (grad,)

def back_keep(v):
    return (v, None)

def back_low(kept, grad):
    return (lower_part(grad),)
lower_part.defvjp(low_keep, low_pass)
low_back.defvjp(back_keep, back_low)

def matmul(former, latter):
    return jnp.dot(former, latter, precision=HIGHEST)

def rms_norm(value_row_set, gain):
    return value_row_set * lax.rsqrt(lax.optimization_barrier(jnp.mean(value_row_set * value_row_set, axis=-1, keepdims=True)) + NORM_EPS) * gain

def apply_rotation(vectors, cosine_table, sine_table):
    half_dim = vectors.shape[-1] // 2
    lower_half = vectors[..., :half_dim]
    upper_half = vectors[..., half_dim:]
    return jnp.concatenate([lower_half * cosine_table - upper_half * sine_table, upper_half * cosine_table + lower_half * sine_table], axis=-1)

def rotary_tables(places):
    frequency = ROPE_BASE ** (-2.0 * jnp.arange(HEAD_SIZE // 2, dtype=jnp.float32) / HEAD_SIZE)
    angles = places.astype(jnp.float32)[:, None] * frequency[None, :]
    return (jnp.cos(angles)[:, None, :], jnp.sin(angles)[:, None, :])

def attend(query_rows, key_row_set, value_row_set, places):
    group_count = QUERY_HEADS // KEY_VALUE_HEADS
    block_length = min(SEQUENCE_TOKENS, 512)
    query_block_set = query_rows.reshape(SEQUENCE_TOKENS // block_length, block_length, KEY_VALUE_HEADS, group_count, HEAD_SIZE)
    place_blocks = places.reshape(SEQUENCE_TOKENS // block_length, block_length)

    def one_block(block_item):
        query_blk, place_blk = block_item
        scores = low_back(ATTN_MULT * jnp.einsum('bgrd,kgd->bgrk', query_blk, key_row_set, precision=HIGHEST))
        allowed = (places[None, :] <= place_blk[:, None])[:, None, None, :]
        weights = jax.nn.softmax(jnp.where(allowed, scores, -jnp.inf), axis=-1)
        return jnp.einsum('bgrk,kgd->bgrd', lower_part(weights), value_row_set, precision=HIGHEST)
    return lax.map(jax.checkpoint(one_block), (query_block_set, place_blocks)).reshape(SEQUENCE_TOKENS, QUERY_HEADS * HEAD_SIZE)

def slot_table(route_rows):
    blocks = route_rows.reshape(N_CONTEXT, ROWS * TOPK)
    names = jnp.arange(EXPERTS, dtype=jnp.int32)
    hits = (blocks[:, :, None] == names[None, None, :]).astype(jnp.int32)
    ranks = lax.optimization_barrier(jnp.sum((jnp.cumsum(hits, axis=1) - hits) * hits, axis=2))
    block_ids = jnp.arange(N_CONTEXT, dtype=jnp.int32)[:, None]
    slots = (blocks * (N_CONTEXT * CAP) + block_ids * CAP + ranks).reshape(SEQUENCE_TOKENS * TOPK).astype(jnp.int32)
    owners = jnp.full((EXPERTS * N_CONTEXT * CAP,), SEQUENCE_TOKENS * TOPK, jnp.int32)
    owners = owners.at[slots].set(jnp.arange(SEQUENCE_TOKENS * TOPK, dtype=jnp.int32))
    return (slots, owners)

def experts(normed, gates, slots, owners, w_gate, w_up, w_down):
    group_width = FF // N_TENSOR
    padded = jnp.concatenate([normed, jnp.zeros((1, MODEL_WIDTH), normed.dtype)], axis=0)
    expert_in = padded[owners // TOPK].reshape(EXPERTS, N_CONTEXT * CAP, MODEL_WIDTH)

    def one_expert(expert_item):
        rows_in, gate_w, up_w, down_w = expert_item
        copies = low_back(jnp.broadcast_to(rows_in[None], (N_TENSOR,) + rows_in.shape))
        gate_pre = low_back(jnp.einsum('gnd,dgf->gnf', copies, gate_w.reshape(MODEL_WIDTH, N_TENSOR, group_width), precision=HIGHEST))
        up_pre = low_back(jnp.einsum('gnd,dgf->gnf', copies, up_w.reshape(MODEL_WIDTH, N_TENSOR, group_width), precision=HIGHEST))
        active = lower_part(jax.nn.silu(gate_pre) * up_pre)
        parts = lower_part(low_back(jnp.einsum('gnf,dgf->gnd', active, down_w.reshape(MODEL_WIDTH, N_TENSOR, group_width), precision=HIGHEST)))
        return lax.optimization_barrier(jnp.sum(parts, axis=0))
    outputs = lax.map(jax.checkpoint(one_expert), (expert_in, w_gate, w_up, w_down))
    chosen = outputs.reshape(EXPERTS * N_CONTEXT * CAP, MODEL_WIDTH)[slots].reshape(SEQUENCE_TOKENS, TOPK, MODEL_WIDTH)
    return jnp.einsum('tk,tkd->td', gates, chosen, precision=HIGHEST)

def forward(resid, params, places, route_rows, slots, owners):
    gain_attn, w_query, w_key, w_value, w_out, gain_moe, w_router, w_gate, w_up, w_down = params
    cosine_table, sine_table = rotary_tables(places)
    normed = lower_part(rms_norm(resid, gain_attn))
    query_lin = low_back(matmul(normed, w_query))
    key_linear = low_back(matmul(normed, w_key))
    value_linear = low_back(matmul(normed, w_value))
    query_rows = lower_part(apply_rotation(query_lin.reshape(SEQUENCE_TOKENS, QUERY_HEADS, HEAD_SIZE), cosine_table, sine_table))
    key_row_set = lower_part(apply_rotation(key_linear.reshape(SEQUENCE_TOKENS, KEY_VALUE_HEADS, HEAD_SIZE), cosine_table, sine_table))
    value_row_set = lower_part(value_linear).reshape(SEQUENCE_TOKENS, KEY_VALUE_HEADS, HEAD_SIZE)
    attended = lower_part(low_back(attend(query_rows, key_row_set, value_row_set, places)))
    attn_out = low_back(matmul(attended, w_out.T))
    middle = resid + RESID_MULT * attn_out
    normed_moe = lower_part(rms_norm(middle, gain_moe))
    logits = low_back(matmul(normed_moe, w_router))
    picked = jnp.take_along_axis(logits, route_rows, axis=1)
    gates = jax.nn.softmax(picked, axis=-1)
    moe_out = experts(normed_moe, gates, slots, owners, w_gate, w_up, w_down)
    return middle + RESID_MULT * moe_out

def reference(hidden_in, positions, routes, out_grad, attn_gain, query_weight, key_matrix, value_matrix, out_weight, moe_gain, router_weight, gate_weight, up_weight, down_weight):
    params = tuple((weight.astype(jnp.float32) for weight in (attn_gain, query_weight, key_matrix, value_matrix, out_weight, moe_gain, router_weight, gate_weight, up_weight, down_weight)))

    def one_sequence(totals, seq_item):
        resid, places, route_rows, grad_rows = seq_item
        slots, owners = slot_table(route_rows)

        def run_layer(inputs, weights):
            return forward(inputs, weights, places, route_rows, slots, owners)
        result, pull_back = jax.vjp(run_layer, resid.astype(jnp.float32), params)
        d_resid, d_params = pull_back(grad_rows.astype(jnp.float32))
        totals = tuple((total + grad for total, grad in zip(totals, d_params)))
        return (totals, (result.astype(jnp.bfloat16), d_resid))
    zeros = tuple((jnp.zeros_like(weight) for weight in params))
    totals, (results, d_inputs) = lax.scan(one_sequence, zeros, (hidden_in, positions, routes, out_grad))
    return (results, d_inputs, totals[0], totals[1], totals[2], totals[3], totals[4], totals[5], totals[6], totals[7], totals[8], totals[9])
```

```python
import functools

import jax
import jax.numpy as jnp
from jax import lax
from jax.experimental import pallas as pl
from jax.experimental.pallas import tpu as pltpu
from jax.sharding import PartitionSpec as P

HEAD_SIZE = 64
NORM_EPS = 1e-06
ATTN_MULT = 0.015625
RESID_MULT = 0.22
ROPE_BASE = 10000.0
F32 = jnp.float32
BF16 = jnp.bfloat16
VMEM_BYTES = 56 * 1024 * 1024
PART_ROWS = 1024
STEPPED = 4


def swap(x, axis, bit):
    devices = lax.axis_size(axis)
    return lax.ppermute(x, axis, [(i, i ^ bit) for i in range(devices)])


def turn(x, steps):
    devices = lax.axis_size("tensor")
    return lax.ppermute(x, "tensor", [(i, (i + steps) % devices) for i in range(devices)])


def take_relative(stack, index):
    order = index ^ jnp.arange(stack.shape[0], dtype=jnp.int32)
    return list(jnp.take(stack, order, axis=0))


def gather_context(x):
    if lax.axis_size("context") > STEPPED:
        return take_relative(lax.all_gather(x, "context"), lax.axis_index("context"))
    blocks = {0: x}
    bit = lax.axis_size("context") // 2
    while bit:
        for m in list(blocks):
            blocks[m | bit] = swap(blocks[m], "context", bit)
        bit //= 2
    return [blocks[m] for m in range(len(blocks))]


def gather_owners(x):
    across = swap(x, "shards", 1)
    return gather_context(x) + gather_context(across)


def scatter_context(blocks, travel):
    if lax.axis_size("context") > STEPPED:
        blocks = take_relative(jnp.stack(blocks), lax.axis_index("context"))
        blocks = jnp.stack(blocks).astype(travel)
        return lax.psum_scatter(blocks, "context", scatter_dimension=0).astype(F32)
    blocks = dict(enumerate(blocks))
    bit, devices = 1, lax.axis_size("context")
    while bit < devices:
        for m in list(blocks):
            if m & bit:
                came = swap(blocks.pop(m).astype(travel), "context", bit)
                blocks[m ^ bit] = blocks[m ^ bit].astype(F32) + came.astype(F32)
        bit *= 2
    return blocks[0]


def scatter_owners(blocks, travel):
    half = len(blocks) // 2
    mine = scatter_context(blocks[:half], travel)
    other = scatter_context(blocks[half:], travel)
    return mine + swap(other.astype(travel), "shards", 1).astype(F32)


def butterfly(x):
    bit = 1
    while bit < lax.axis_size("tensor"):
        x = x + lax.ppermute(x, "tensor", [(i, i ^ bit) for i in range(lax.axis_size("tensor"))])
        bit *= 2
    return x


def xor_blocks(pieces, index):
    if len(pieces) > 2 * STEPPED:
        return take_relative(jnp.stack(pieces), index)
    pieces, bit = list(pieces), 1
    while bit < len(pieces):
        flag = (index & bit) != 0
        pieces = [jnp.where(flag, pieces[i ^ bit], pieces[i]) for i in range(len(pieces))]
        bit *= 2
    return pieces


def cut(x, index, size):
    return lax.dynamic_slice_in_dim(x, index * size, size, axis=0)


def scatter_tensor(x, travel):
    devices, me = lax.axis_size("tensor"), lax.axis_index("tensor")
    size = x.shape[0] // devices
    total = cut(x, me, size).astype(F32)
    for k in range(1, devices):
        part = cut(x, (me + k) % devices, size).astype(travel)
        total = total + turn(part, k).astype(F32)
    return total


def place_quarters(pieces, indices):
    size = pieces[0].shape[0]
    whole = jnp.zeros((size * len(pieces),) + pieces[0].shape[1:], pieces[0].dtype)
    for piece, index in zip(pieces, indices):
        whole = lax.dynamic_update_slice_in_dim(whole, piece, index * size, axis=0)
    return whole


def gather_tensor(x):
    devices, me = lax.axis_size("tensor"), lax.axis_index("tensor")
    pieces = [x] + [turn(x, k) for k in range(1, devices)]
    return place_quarters(pieces, [(me - k) % devices for k in range(devices)])


def nn(a, b):
    return lax.dot_general(a, b, (((1,), (0,)), ((), ())), preferred_element_type=F32)


def tn(a, b):
    return lax.dot_general(a, b, (((0,), (0,)), ((), ())), preferred_element_type=F32)


def nt(a, b):
    return lax.dot_general(a, b, (((1,), (1,)), ((), ())), preferred_element_type=F32)


def vmem():
    return pl.BlockSpec(memory_space=pltpu.VMEM)


def rotate(x, cosine, sine):
    lanes = x.shape[1]
    times = lanes // cosine.shape[1]
    lane = lax.broadcasted_iota(jnp.int32, x.shape, 1)
    half = HEAD_SIZE // 2
    partner = jnp.where(
        lane % HEAD_SIZE < half, pltpu.roll(x, lanes - half, 1), pltpu.roll(x, half, 1)
    )
    return x * jnp.concatenate([cosine] * times, 1) + partner * jnp.concatenate([sine] * times, 1)


def project_kernel(wide, narrow, hid_ref, gain_ref, w_ref, cos_ref, sin_ref, norm_ref, q_ref, kv_ref):
    hid = hid_ref[...].astype(F32)
    scale = lax.rsqrt(jnp.mean(hid * hid, axis=1, keepdims=True) + NORM_EPS)
    normed = (hid * scale * gain_ref[...]).astype(BF16)
    norm_ref[...] = normed
    lin = nn(normed, w_ref[...])
    turned = rotate(lin[:, : wide + narrow], cos_ref[...], sin_ref[...]).astype(BF16)
    q_ref[...] = turned[:, :wide] * ATTN_MULT
    kv_ref[:, :narrow] = turned[:, wide:]
    kv_ref[:, narrow:] = lin[:, wide + narrow :].astype(BF16)


def project(hidden, gain, weights, cosine, sine, wide, narrow):
    rows, width = hidden.shape
    return pl.pallas_call(
        functools.partial(project_kernel, wide, narrow),
        out_shape=(
            jax.ShapeDtypeStruct((rows, width), BF16),
            jax.ShapeDtypeStruct((rows, wide), BF16),
            jax.ShapeDtypeStruct((rows, 2 * narrow), BF16),
        ),
        in_specs=[vmem()] * 5,
        out_specs=(vmem(),) * 3,
        compiler_params=pltpu.CompilerParams(vmem_limit_bytes=VMEM_BYTES),
        name="project",
    )(hidden, gain, weights, cosine, sine)


def attend_kernel(heads, group, q_ref, kv_ref, own_ref, all_ref, out_ref, lse_ref):
    narrow = kv_ref.shape[1] // 2
    bias = jnp.where(all_ref[...] <= own_ref[...], 0.0, -1e30)
    for h in range(heads):
        at, kv_at = h * HEAD_SIZE, (h // group) * HEAD_SIZE
        key = kv_ref[:, kv_at : kv_at + HEAD_SIZE]
        value = kv_ref[:, narrow + kv_at : narrow + kv_at + HEAD_SIZE]
        scores = nt(q_ref[:, at : at + HEAD_SIZE], key) + bias
        top = jnp.max(scores, axis=1, keepdims=True)
        weights = jnp.exp(scores - top)
        total = jnp.sum(weights, axis=1, keepdims=True)
        out = nn(weights.astype(BF16), value) / total
        out_ref[:, at : at + HEAD_SIZE] = out.astype(BF16)
        lse_ref[:, h : h + 1] = top + jnp.log(total)


def attend(query, kv, own_places, all_places, heads, group):
    rows = query.shape[0]
    return pl.pallas_call(
        functools.partial(attend_kernel, heads, group),
        out_shape=(
            jax.ShapeDtypeStruct(query.shape, BF16),
            jax.ShapeDtypeStruct((rows, heads), F32),
        ),
        in_specs=[vmem()] * 4,
        out_specs=(vmem(),) * 2,
        compiler_params=pltpu.CompilerParams(vmem_limit_bytes=VMEM_BYTES),
        name="attend",
    )(query, kv, own_places, all_places)


def attend_back_kernel(
    heads, group, q_ref, kv_ref, own_ref, all_ref, lse_ref, grad_ref, cos_ref, sin_ref, dq_ref, dkv_ref
):
    narrow = kv_ref.shape[1] // 2
    bias = jnp.where(all_ref[...] <= own_ref[...], 0.0, -1e30)
    d_queries = []
    for pair in range(heads // group):
        kv_at = pair * HEAD_SIZE
        key = kv_ref[:, kv_at : kv_at + HEAD_SIZE]
        value = kv_ref[:, narrow + kv_at : narrow + kv_at + HEAD_SIZE]
        d_key, d_value = 0.0, 0.0
        for h in range(pair * group, (pair + 1) * group):
            at = h * HEAD_SIZE
            query, grad = q_ref[:, at : at + HEAD_SIZE], grad_ref[:, at : at + HEAD_SIZE]
            probs = jnp.exp(nt(query, key) + bias - lse_ref[:, h : h + 1])
            d_probs = nt(grad, value)
            delta = jnp.sum(probs * d_probs, axis=1, keepdims=True)
            d_scores = (probs * (d_probs - delta)).astype(BF16)
            d_queries.append(nn(d_scores, key) * ATTN_MULT)
            d_key = d_key + tn(d_scores, query)
            d_value = d_value + tn(probs.astype(BF16), grad)
        dkv_ref[:, kv_at : kv_at + HEAD_SIZE] = d_key.astype(BF16)
        dkv_ref[:, narrow + kv_at : narrow + kv_at + HEAD_SIZE] = d_value.astype(BF16)
    d_query = jnp.concatenate(d_queries, axis=1)
    dq_ref[...] = rotate(d_query, cos_ref[...], -sin_ref[...]).astype(BF16)


def attend_back(query, kv, own_places, all_places, lse, grad, cosine, sine, heads, group):
    return pl.pallas_call(
        functools.partial(attend_back_kernel, heads, group),
        out_shape=(
            jax.ShapeDtypeStruct(query.shape, BF16),
            jax.ShapeDtypeStruct(kv.shape, BF16),
        ),
        in_specs=[vmem()] * 8,
        out_specs=(vmem(),) * 2,
        compiler_params=pltpu.CompilerParams(vmem_limit_bytes=VMEM_BYTES),
        name="attend_back",
    )(query, kv, own_places, all_places, lse, grad, cosine, sine)


def experts_kernel(
    pair,
    x_ref,
    g_ref,
    gates_ref,
    place_ref,
    wg0_ref,
    wg1_ref,
    wu0_ref,
    wu1_ref,
    wd0_ref,
    wd1_ref,
    out_ref,
    din_ref,
    dgates_ref,
    dwg0_ref,
    dwg1_ref,
    dwu0_ref,
    dwu1_ref,
    dwd0_ref,
    dwd1_ref,
    out_acc,
    din_acc,
):
    step, steps = pl.program_id(0), pl.num_programs(0)
    first = place_ref[0] == 0
    base = place_ref[1] + step * pair
    units = wg0_ref.shape[2]

    def whole(own_ref, other_ref):
        own = jnp.concatenate([own_ref[i] for i in range(pair)], axis=1)
        other = jnp.concatenate([other_ref[i] for i in range(pair)], axis=1)
        return jnp.concatenate(
            [jnp.where(first, own, other), jnp.where(first, other, own)], axis=0
        )

    def halves(grad, own_ref, other_ref):
        half = grad.shape[0] // 2
        own = jnp.where(first, grad[:half], grad[half:]).astype(BF16)
        other = jnp.where(first, grad[half:], grad[:half]).astype(BF16)
        for i in range(pair):
            own_ref[i] = own[:, i * units : (i + 1) * units]
            other_ref[i] = other[:, i * units : (i + 1) * units]

    rows_in, rows_grad, gates = x_ref[...], g_ref[...], gates_ref[...]
    w_gate, w_up, w_down = whole(wg0_ref, wg1_ref), whole(wu0_ref, wu1_ref), whole(wd0_ref, wd1_ref)
    lane = lax.broadcasted_iota(jnp.int32, gates.shape, 1)
    columns = [
        jnp.sum(jnp.where(lane == base + i, gates, 0.0), axis=1, keepdims=True) for i in range(pair)
    ]
    wide = jnp.concatenate(
        [jnp.broadcast_to(column, (gates.shape[0], units)) for column in columns], axis=1
    )
    gate_pre, up_pre = nn(rows_in, w_gate), nn(rows_in, w_up)
    sigma = 1.0 / (1.0 + jnp.exp(-gate_pre))
    silu_gate = gate_pre * sigma
    active = silu_gate * up_pre
    hidden = (wide * active).astype(BF16)
    raw = nn(rows_grad, w_down)
    product = raw * active
    d_gates = jnp.zeros_like(gates)
    for i in range(pair):
        column = RESID_MULT * jnp.sum(product[:, i * units : (i + 1) * units], axis=1, keepdims=True)
        d_gates = jnp.where(lane == base + i, column, d_gates)
    d_active = (RESID_MULT * wide) * raw
    d_gate_pre = (d_active * up_pre * sigma * (1.0 + gate_pre * (1.0 - sigma))).astype(BF16)
    d_up_pre = (d_active * silu_gate).astype(BF16)
    out = nt(hidden, w_down)
    d_in = nt(d_gate_pre, w_gate) + nt(d_up_pre, w_up)

    @pl.when(step == 0)
    def _():
        out_acc[...] = out
        din_acc[...] = d_in
        dgates_ref[...] = d_gates

    @pl.when(step > 0)
    def _():
        out_acc[...] += out
        din_acc[...] += d_in
        dgates_ref[...] += d_gates

    @pl.when(step == steps - 1)
    def _():
        out_ref[...] = out_acc[...].astype(BF16)
        din_ref[...] = din_acc[...].astype(BF16)

    halves(tn(rows_in, d_gate_pre), dwg0_ref, dwg1_ref)
    halves(tn(rows_in, d_up_pre), dwu0_ref, dwu1_ref)
    halves(RESID_MULT * tn(rows_grad, hidden), dwd0_ref, dwd1_ref)


def run_experts(rows_in, rows_grad, gates, place, weights):
    tokens, width = rows_in.shape
    count, half, units = weights[0].shape
    pair = 2 if count % 2 == 0 else 1
    fixed = lambda i: (0, 0)
    moving = pl.BlockSpec((pair, half, units), lambda i: (i, 0, 0))
    return pl.pallas_call(
        functools.partial(experts_kernel, pair),
        grid=(count // pair,),
        out_shape=(
            jax.ShapeDtypeStruct((tokens, width), BF16),
            jax.ShapeDtypeStruct((tokens, width), BF16),
            jax.ShapeDtypeStruct(gates.shape, F32),
        )
        + (jax.ShapeDtypeStruct((count, half, units), BF16),) * 6,
        in_specs=[
            pl.BlockSpec((tokens, width), fixed),
            pl.BlockSpec((tokens, width), fixed),
            pl.BlockSpec(gates.shape, fixed),
            pl.BlockSpec(memory_space=pltpu.SMEM),
        ]
        + [moving] * 6,
        out_specs=(
            pl.BlockSpec((tokens, width), fixed),
            pl.BlockSpec((tokens, width), fixed),
            pl.BlockSpec(gates.shape, fixed),
        )
        + (moving,) * 6,
        scratch_shapes=[pltpu.VMEM((tokens, width), F32), pltpu.VMEM((tokens, width), F32)],
        compiler_params=pltpu.CompilerParams(vmem_limit_bytes=VMEM_BYTES),
        name="experts",
    )(rows_in, rows_grad, gates, place, *weights)


def rms_back(rows, gain, grad):
    scale = lax.rsqrt(jnp.mean(rows * rows, axis=-1, keepdims=True) + NORM_EPS)
    d_gain = jnp.sum(grad * rows * scale, axis=0)
    pulled = grad * gain
    mean = jnp.mean(pulled * rows, axis=-1, keepdims=True)
    return scale * pulled - rows * (scale * scale * scale) * mean, d_gain


def body(
    hidden_in,
    positions,
    routes,
    out_grad,
    attn_gain,
    query_weight,
    key_matrix,
    value_matrix,
    out_weight,
    moe_gain,
    router_weight,
    gate_weight,
    up_weight,
    down_weight,
):
    shards, contexts, tensors = (lax.axis_size(a) for a in ("shards", "context", "tensor"))
    shard, context, tensor = (lax.axis_index(a) for a in ("shards", "context", "tensor"))
    owner, owners = shard * contexts + context, shards * contexts
    rows, width = hidden_in.shape[1:]
    chunk = width // owners
    quarter = rows // tensors
    wide, narrow = query_weight.shape[1], key_matrix.shape[1]
    heads, group = wide // HEAD_SIZE, wide // narrow
    expert_count, local_experts = router_weight.shape[1], gate_weight.shape[0]
    columns = wide + 2 * narrow

    small = jnp.concatenate(
        [
            jnp.pad(
                jnp.concatenate([attn_gain, moe_gain])[None], ((0, 7), (0, columns - 2 * chunk))
            ),
            jnp.pad(
                router_weight.reshape(8, chunk * expert_count // 8),
                ((0, 0), (0, columns - chunk * expert_count // 8)),
            ),
        ],
        axis=0,
    )
    packed = jnp.concatenate(
        [jnp.concatenate([query_weight, key_matrix, value_matrix], axis=1), small], axis=0
    )
    pieces = gather_owners(packed)
    w_qkv = jnp.concatenate([p[:chunk] for p in pieces], axis=0)
    gain_a = jnp.concatenate([p[chunk : chunk + 1, :chunk] for p in pieces], axis=1).astype(F32)
    gain_m_pieces = [p[chunk : chunk + 1, chunk : 2 * chunk] for p in pieces]
    router_pieces = [p[chunk + 8 : chunk + 16, : chunk * expert_count // 8] for p in pieces]
    gain_m = jnp.concatenate(xor_blocks(gain_m_pieces, owner), axis=1).astype(F32)
    w_router = jnp.concatenate(
        [p.reshape(chunk, expert_count) for p in xor_blocks(router_pieces, owner)], axis=0
    )

    place_all = positions[0].reshape(contexts, rows)
    place_blocks = [place_all[i] for i in range(contexts)]
    place_blocks = xor_blocks(place_blocks, context)
    own_places = place_blocks[0].reshape(rows, 1)
    all_places = jnp.concatenate(place_blocks).reshape(1, contexts * rows)
    half = HEAD_SIZE // 2
    frequency = ROPE_BASE ** (-2.0 * jnp.arange(half, dtype=F32) / HEAD_SIZE)
    angles = own_places.astype(F32) * frequency[None, :]
    cosine, sine = jnp.cos(angles), jnp.sin(angles)
    cosine = jnp.concatenate([cosine] * 4, axis=1)
    sine = jnp.concatenate([-sine, sine] * 2, axis=1)

    hidden = hidden_in[0]
    hidden_rel = jnp.concatenate(
        xor_blocks([hidden[:, i * chunk : (i + 1) * chunk] for i in range(owners)], owner), axis=1
    )
    normed_a, query, kv = project(hidden_rel, gain_a, w_qkv, cosine, sine, wide, narrow)
    kv_all = jnp.concatenate(gather_context(kv), axis=0)
    attended, lse = attend(query, kv_all, own_places, all_places, heads, group)

    out_own = jnp.concatenate([out_weight] + [turn(out_weight, k) for k in range(1, tensors)], axis=1)
    w_out = jnp.concatenate(xor_blocks(gather_owners(out_own), owner), axis=0)
    attended_all = jnp.concatenate(
        [attended] + [turn(attended, k) for k in range(1, tensors)], axis=1
    )
    middle = hidden.astype(F32) + RESID_MULT * nt(attended_all, w_out)
    scale = lax.rsqrt(jnp.mean(middle * middle, axis=-1, keepdims=True) + NORM_EPS)
    normed_m = (middle * scale * gain_m).astype(BF16)

    rows_in = jnp.concatenate(gather_context(normed_m), axis=0)
    rows_grad = jnp.concatenate(gather_context(out_grad[0]), axis=0)
    routes_all = jnp.concatenate(gather_context(routes[0].T), axis=1)
    names = jnp.arange(expert_count, dtype=jnp.int32)
    mask = jnp.any(routes_all[:, :, None] == names[None, None, :], axis=0)
    logits = jnp.where(mask, nn(rows_in, w_router), -1e30)
    gates = jnp.where(mask, jnp.exp(logits - jnp.max(logits, axis=-1, keepdims=True)), 0.0)
    gates = gates / jnp.sum(gates, axis=-1, keepdims=True)
    others = [swap(w, "shards", 1) for w in (gate_weight, up_weight, down_weight)]
    place = jnp.stack([shard, context * local_experts]).astype(jnp.int32)
    weights = (gate_weight, others[0], up_weight, others[1], down_weight, others[2])
    size = min(rows_in.shape[0], PART_ROWS)
    parts = [
        run_experts(cut(rows_in, i, size), cut(rows_grad, i, size), cut(gates, i, size), place, weights)
        for i in range(rows_in.shape[0] // size)
    ]
    out_part, din_part, dgates_part = (
        jnp.concatenate([p[i] for p in parts], axis=0) for i in range(3)
    )
    dwg0, dwg1, dwu0, dwu1, dwd0, dwd1 = (
        sum([p[i].astype(F32) for p in parts[1:]], parts[0][i]) for i in range(3, 9)
    )
    expert_grads = [
        own.astype(F32) + swap(other.astype(BF16), "shards", 1).astype(F32)
        for own, other in ((dwg0, dwg1), (dwu0, dwu1), (dwd0, dwd1))
    ]

    def blocks_of(x):
        return [x[m * rows : (m + 1) * rows] for m in range(contexts)]

    d_gates = scatter_context([b.T for b in blocks_of(dgates_part)], F32)
    d_gates = d_gates + sum(turn(d_gates, k) for k in range(1, tensors))
    d_gates = cut(d_gates.T, tensor, quarter)
    d_normed = scatter_tensor(scatter_context(blocks_of(din_part), BF16), BF16)
    gates_q = cut(gates[:rows], tensor, quarter)
    d_picked = gates_q * (d_gates - jnp.sum(gates_q * d_gates, axis=-1, keepdims=True))
    d_logits = d_picked.astype(BF16)
    d_normed = d_normed + nt(d_logits, w_router)
    middle_q = cut(middle, tensor, quarter)
    d_router = tn(cut(normed_m, tensor, quarter), d_logits)
    d_rows, d_gain_m = rms_back(middle_q, gain_m, d_normed)
    d_middle = cut(out_grad[0], tensor, quarter).astype(F32) + d_rows
    d_attn = (RESID_MULT * d_middle).astype(BF16)

    d_attended = nn(d_attn, w_out).astype(BF16)
    pieces = [
        turn(d_attended[:, k * wide : (k + 1) * wide], -k) if k else d_attended[:, :wide]
        for k in range(tensors)
    ]
    d_attended = place_quarters(pieces, [(tensor + k) % tensors for k in range(tensors)])
    d_query, d_kv = attend_back(
        query, kv_all, own_places, all_places, lse, d_attended, cosine, sine, heads, group
    )
    d_kv = scatter_context(blocks_of(d_kv), BF16)
    d_key = d_kv[:, :narrow]
    halves = d_key.reshape(rows, narrow // HEAD_SIZE, 2, half)
    turned = jnp.stack([halves[:, :, 1], halves[:, :, 0]], axis=2).reshape(rows, narrow)
    d_key = d_key * cosine[:, :narrow] - turned * sine[:, :narrow]
    d_lin = jnp.concatenate(
        [d_query, d_key.astype(BF16), d_kv[:, narrow:].astype(BF16)], axis=1
    )
    d_normed_a = scatter_tensor(nt(d_lin, w_qkv), BF16)
    d_rows, d_gain_a = rms_back(
        cut(hidden_rel, tensor, quarter).astype(F32), gain_a, d_normed_a
    )
    d_rows = jnp.concatenate(
        xor_blocks([d_rows[:, i * chunk : (i + 1) * chunk] for i in range(owners)], owner), axis=1
    )
    in_grad = gather_tensor((d_middle + d_rows).astype(BF16)).astype(F32)

    moe_out = scatter_tensor(scatter_context(blocks_of(out_part), BF16), BF16)
    block_out = gather_tensor((middle_q + RESID_MULT * moe_out).astype(BF16))

    d_w_qkv = tn(normed_a, d_lin).astype(BF16)
    d_qkv = scatter_owners([d_w_qkv[i * chunk : (i + 1) * chunk] for i in range(owners)], BF16)
    d_w_out = tn(gather_tensor(d_attn), attended).astype(BF16)
    d_out = scatter_owners(
        xor_blocks([d_w_out[i * chunk : (i + 1) * chunk] for i in range(owners)], owner), BF16
    )
    gain_a_pieces = [d_gain_a[i * chunk : (i + 1) * chunk] for i in range(owners)]
    gain_m_pieces = xor_blocks([d_gain_m[i * chunk : (i + 1) * chunk] for i in range(owners)], owner)
    router_pieces = xor_blocks([d_router[i * chunk : (i + 1) * chunk] for i in range(owners)], owner)
    small = [
        jnp.concatenate([a[None], m[None], r.T], axis=0)
        for a, m, r in zip(gain_a_pieces, gain_m_pieces, router_pieces)
    ]
    small = butterfly(jnp.concatenate(small, axis=1))
    small = scatter_owners([small[:, i * chunk : (i + 1) * chunk] for i in range(owners)], F32)
    return (
        block_out[None],
        in_grad[None],
        small[0],
        d_qkv[:, :wide],
        d_qkv[:, wide : wide + narrow],
        d_qkv[:, wide + narrow :],
        d_out,
        small[1],
        small[2:].T,
        expert_grads[0],
        expert_grads[1],
        expert_grads[2],
    )


def solution(mesh):
    owned = ("shards", "context")
    rows = P("shards", "context", None)
    split = P(owned, "tensor")
    expert = P("context", "shards", "tensor")
    return jax.shard_map(
        body,
        mesh=mesh,
        in_specs=(
            rows,
            P("shards", None),
            rows,
            rows,
            P(owned),
            split,
            split,
            split,
            split,
            P(owned),
            P(owned, None),
            expert,
            expert,
            expert,
        ),
        out_specs=(
            rows,
            rows,
            P(owned),
            split,
            split,
            split,
            split,
            P(owned),
            P(owned, None),
            expert,
            expert,
            expert,
        ),
        check_vma=False,
    )
```

```python
import functools

import jax
import jax.numpy as jnp
from jax import lax
from jax.experimental import pallas as pl
from jax.experimental.pallas import tpu as pltpu
from jax.sharding import PartitionSpec as P

HEAD_SIZE = 64
NORM_EPS = 1e-06
ATTN_MULT = 0.015625
RESID_MULT = 0.22
ROPE_BASE = 10000.0
F32 = jnp.float32
BF16 = jnp.bfloat16
VMEM_BYTES = 56 * 1024 * 1024
PART_ROWS = 1024
LANES = 128


def swap(x, axis, bit):
    devices = lax.axis_size(axis)
    return lax.ppermute(x, axis, [(i, i ^ bit) for i in range(devices)])


def turn(x, steps):
    devices = lax.axis_size("tensor")
    return lax.ppermute(x, "tensor", [(i, (i + steps) % devices) for i in range(devices)])


def stepped():
    return lax.axis_size("context") == 4 and lax.axis_size("shards") == 2


def after(x, *others):
    return lax.optimization_barrier((x,) + others)[0]


def gather_context(x):
    if not stepped():
        return [lax.all_gather(x, "context", axis=0, tiled=True)]
    across = swap(x, "context", 2)
    return [x, swap(x, "context", 1), across, swap(across, "context", 1)]


def gather_owners(x):
    if not stepped():
        return [lax.all_gather(x, ("shards", "context"))]
    far = []
    for m in (2, 4, 6):
        far.append(lax.ppermute(x, ("shards", "context"), [(i, i ^ m) for i in range(8)]))
    near = swap(x, "context", 1)
    odd = swap(jnp.concatenate(far, axis=0), "context", 1)
    size = x.shape[0]
    return [x] + far + [near] + [odd[i * size : (i + 1) * size] for i in range(3)]


OWNER_ORDER = (0, 4, 2, 6, 1, 5, 3, 7)


def scatter_owners(keep, send, travel):
    size = keep.shape[0] // 4
    total = keep.astype(F32) + swap(send.astype(travel), "context", 1).astype(F32)
    far = swap(total[2 * size :].astype(travel), "context", 2).astype(F32)
    total = total[: 2 * size] + far
    return total, total[:size] + swap(total[size:].astype(travel), "shards", 1).astype(F32)


def butterfly(x):
    bit = 1
    while bit < lax.axis_size("tensor"):
        x = x + lax.ppermute(x, "tensor", [(i, i ^ bit) for i in range(lax.axis_size("tensor"))])
        bit *= 2
    return x


def xor_blocks(pieces, index):
    pieces, bit = list(pieces), 1
    while bit < len(pieces):
        flag = (index & bit) != 0
        pieces = [jnp.where(flag, pieces[i ^ bit], pieces[i]) for i in range(len(pieces))]
        bit *= 2
    return pieces


def columns_of(x, count):
    size = x.shape[1] // count
    return [x[:, i * size : (i + 1) * size] for i in range(count)]


def cut(x, index, size):
    return lax.dynamic_slice_in_dim(x, index * size, size, axis=0)


def gather_tensor(x):
    devices, me = lax.axis_size("tensor"), lax.axis_index("tensor")
    size = x.shape[0]
    whole = jnp.zeros((size * devices,) + x.shape[1:], x.dtype)
    for k in range(devices):
        piece = turn(x, k) if k else x
        whole = lax.dynamic_update_slice_in_dim(whole, piece, (me - k) % devices * size, axis=0)
    return whole


def nn(a, b):
    return lax.dot_general(a, b, (((1,), (0,)), ((), ())), preferred_element_type=F32)


def tn(a, b):
    return lax.dot_general(a, b, (((0,), (0,)), ((), ())), preferred_element_type=F32)


def nt(a, b):
    return lax.dot_general(a, b, (((1,), (1,)), ((), ())), preferred_element_type=F32)


def vmem():
    return pl.BlockSpec(memory_space=pltpu.VMEM)


def rotate(x, cosine, sine):
    lanes = x.shape[1]
    times = lanes // cosine.shape[1]
    lane = lax.broadcasted_iota(jnp.int32, x.shape, 1)
    half = HEAD_SIZE // 2
    partner = jnp.where(
        lane % HEAD_SIZE < half, pltpu.roll(x, lanes - half, 1), pltpu.roll(x, half, 1)
    )
    return x * jnp.concatenate([cosine] * times, 1) + partner * jnp.concatenate([sine] * times, 1)


def call(kernel, out_shape, operands, name, smem=(), **more):
    specs = [pl.BlockSpec(memory_space=pltpu.SMEM)] * len(smem) + [vmem()] * len(operands)
    return pl.pallas_call(
        kernel,
        out_shape=tuple(out_shape),
        in_specs=specs,
        out_specs=(vmem(),) * len(out_shape),
        compiler_params=pltpu.CompilerParams(vmem_limit_bytes=VMEM_BYTES),
        name=name,
        **more,
    )(*smem, *operands)


def shape(dims, dtype):
    return jax.ShapeDtypeStruct(tuple(dims), dtype)


def project_kernel(wide, narrow, chunk, hid_ref, gain_ref, cos_ref, sin_ref, *refs):
    *pieces, norm_ref, q_ref, kv_ref, w_ref = refs
    for i, piece in enumerate(pieces):
        w_ref[i * chunk : (i + 1) * chunk] = piece[:chunk, : w_ref.shape[1]]
    hid = hid_ref[...].astype(F32)
    scale = lax.rsqrt(jnp.mean(hid * hid, axis=1, keepdims=True) + NORM_EPS)
    normed = (hid * scale * gain_ref[...]).astype(BF16)
    norm_ref[...] = normed
    lin = nn(normed, w_ref[...])
    turned = rotate(lin[:, : wide + narrow], cos_ref[...], sin_ref[...]).astype(BF16)
    q_ref[...] = turned[:, :wide] * ATTN_MULT
    kv_ref[:, :narrow] = turned[:, wide:]
    kv_ref[:, narrow:] = lin[:, wide + narrow :].astype(BF16)


def project(hidden, gain, pieces, cosine, sine, wide, narrow, chunk):
    rows, width = hidden.shape
    return call(
        functools.partial(project_kernel, wide, narrow, chunk),
        (
            shape((rows, width), BF16),
            shape((rows, wide), BF16),
            shape((rows, 2 * narrow), BF16),
            shape((width, wide + 2 * narrow), BF16),
        ),
        (hidden, gain, cosine, sine, *pieces),
        "project",
    )


def assemble_kernel(order, chunk, place_ref, odd_ref, *refs):
    *even_refs, out_ref = refs
    size, wide = even_refs[0].shape
    for k, even_ref in enumerate(even_refs):
        for at, r in enumerate(order):
            start = at % (len(order) // 2) * chunk
            rows = pl.ds(pl.multiple_of((place_ref[3] ^ r) * chunk, chunk), chunk)
            source = odd_ref if r % 2 else even_ref
            start += k * size if r % 2 else 0
            out_ref[rows, k * wide : (k + 1) * wide] = source[start : start + chunk]


def middle_kernel(hid_ref, gain_ref, w_ref, *refs):
    *att_refs, mid_ref, norm_ref = refs
    attended = jnp.concatenate([r[...] for r in att_refs], axis=1)
    middle = hid_ref[...].astype(F32) + RESID_MULT * nt(attended, w_ref[...])
    scale = lax.rsqrt(jnp.mean(middle * middle, axis=1, keepdims=True) + NORM_EPS)
    mid_ref[...] = middle
    norm_ref[...] = (middle * scale * gain_ref[...]).astype(BF16)


def split_lanes(x):
    high = x.astype(BF16)
    low = (x - high.astype(F32)).astype(BF16).astype(F32)
    return (high.astype(F32) + pltpu.roll(low, LANES // 2, 1)).astype(BF16)


def join_lanes(x):
    lane = lax.broadcasted_iota(jnp.int32, x.shape, 1)
    return jnp.where(lane < LANES // 2, x + pltpu.roll(x, LANES // 2, 1), 0.0)


def fold_kernel(width, quarters, terms, place_ref, *refs):
    total = refs[0][...].astype(F32)
    for ref in refs[1:terms]:
        total = total + ref[...].astype(F32)
    if not quarters:
        ref = refs[terms]
        ref[:, :width] = total[:, :width].astype(BF16)
        if total.shape[1] > width:
            ref[:, width:] = split_lanes(join_lanes(total[:, width:]))
        return
    own_ref, *send_refs, total_ref = refs[terms:]
    if total.shape[1] > width:
        total = jnp.concatenate([total[:, :width], join_lanes(total[:, width:])], axis=1)
    total_ref[...] = total
    size = own_ref.shape[0]

    def part(index):
        index = lax.rem(place_ref[4] + index, quarters)
        return total_ref[pl.ds(pl.multiple_of(index * size, size), size)]

    own_ref[...] = part(0)
    for k, ref in enumerate(send_refs, 1):
        found = part(k)
        ref[:, :width] = found[:, :width].astype(BF16)
        if found.shape[1] > width:
            ref[:, width:] = split_lanes(found[:, width:])


def fold(terms, place, width, quarters):
    rows, lanes = terms[0].shape
    size = rows // max(quarters, 1)
    outs = [shape((size, lanes), BF16)]
    if quarters:
        outs = [shape((size, lanes), F32)] + outs * (quarters - 1)
    return call(
        functools.partial(fold_kernel, width, quarters, len(terms)),
        outs,
        terms,
        "fold",
        smem=(place,),
        scratch_shapes=[pltpu.VMEM((rows, lanes), F32)] if quarters else [],
    )


def middle_back_kernel(width, _place_ref, mid_ref, norm_ref, gain_ref, grad_ref, gates_ref, router_ref, w_ref, *refs):
    outs = (len(refs) - 4) // 2
    parts, (dmid_ref, dattn_ref, dgain_ref, drouter_ref) = refs[:outs], refs[outs : outs + 4]
    total = parts[0][...]
    for part in parts[1:]:
        total = total + part[...].astype(F32)
    gates, d_gates = gates_ref[...], join_lanes(total[:, width:])
    d_picked = gates * (d_gates - jnp.sum(gates * d_gates, axis=1, keepdims=True))
    d_logits = d_picked.astype(BF16)
    drouter_ref[...] = tn(norm_ref[...], d_logits)
    d_normed = total[:, :width] + nt(d_logits, router_ref[...])
    d_rows, d_gain = rms_back(mid_ref[...], gain_ref[...], d_normed)
    d_middle = grad_ref[...].astype(F32) + d_rows
    d_attn = (RESID_MULT * d_middle).astype(BF16)
    dmid_ref[...], dattn_ref[...], dgain_ref[...] = d_middle, d_attn, d_gain
    d_attended = nn(d_attn, w_ref[...]).astype(BF16)
    wide = d_attended.shape[1] // outs
    for k, ref in enumerate(refs[outs + 4 :]):
        ref[...] = d_attended[:, k * wide : (k + 1) * wide]


def project_back_kernel(narrow, place_ref, dq_ref, keep_ref, came_ref, cos_ref, sin_ref, w_ref, *refs):
    own_ref, *send_refs, dlin_ref, total_ref = refs
    d_kv = keep_ref[...].astype(F32) + came_ref[...].astype(F32)
    d_key = rotate(d_kv[:, :narrow], cos_ref[...], -sin_ref[...])
    d_lin = jnp.concatenate(
        [dq_ref[...], d_key.astype(BF16), d_kv[:, narrow:].astype(BF16)], axis=1
    )
    dlin_ref[...] = d_lin
    total_ref[...] = nt(d_lin, w_ref[...])
    size, quarters = own_ref.shape[0], 1 + len(send_refs)

    def part(k):
        index = lax.rem(place_ref[4] + k, quarters)
        return total_ref[pl.ds(pl.multiple_of(index * size, size), size)]

    own_ref[...] = part(0)
    for k, ref in enumerate(send_refs, 1):
        ref[...] = part(k).astype(BF16)


def weights_back_kernel(order, chunk, place_ref, norm_ref, dlin_ref, dattn_ref, att_ref, keep_ref, send_ref, scratch_ref):
    lin = tn(norm_ref[...], dlin_ref[...]).astype(BF16)
    scratch_ref[...] = tn(dattn_ref[...], att_ref[...])
    split = lin.shape[1]
    for at, r in enumerate(order):
        ref = (keep_ref, send_ref)[r % 2]
        start = at % (len(order) // 2) * chunk
        rows = pl.ds(pl.multiple_of((place_ref[3] ^ r) * chunk, chunk), chunk)
        ref[start : start + chunk, :split] = lin[r * chunk : (r + 1) * chunk]
        ref[start : start + chunk, split:] = scratch_ref[rows].astype(BF16)


def whole_of(refs):
    return jnp.concatenate([r[...] for r in refs], axis=0) if len(refs) > 1 else refs[0][...]


def attend_kernel(heads, group, q_ref, own_ref, all_ref, *refs):
    *kv_refs, out_ref, lse_ref = refs
    kv = whole_of(kv_refs)
    narrow = kv.shape[1] // 2
    bias = jnp.where(all_ref[...] <= own_ref[...], 0.0, -1e30)
    for h in range(heads):
        at, kv_at = h * HEAD_SIZE, (h // group) * HEAD_SIZE
        key = kv[:, kv_at : kv_at + HEAD_SIZE]
        value = kv[:, narrow + kv_at : narrow + kv_at + HEAD_SIZE]
        scores = nt(q_ref[:, at : at + HEAD_SIZE], key) + bias
        top = jnp.max(scores, axis=1, keepdims=True)
        weights = jnp.exp(scores - top)
        total = jnp.sum(weights, axis=1, keepdims=True)
        out = nn(weights.astype(BF16), value) / total
        out_ref[:, at : at + HEAD_SIZE] = out.astype(BF16)
        lse_ref[:, h : h + 1] = top + jnp.log(total)


def attend(query, kv, own_places, all_places, heads, group):
    return call(
        functools.partial(attend_kernel, heads, group),
        (shape(query.shape, BF16), shape((query.shape[0], heads), F32)),
        (query, own_places, all_places, *kv),
        "attend",
    )


def attend_back_kernel(
    heads, group, quarters, blocks, place_ref, q_ref, own_ref, all_ref, lse_ref, cos_ref, sin_ref, *refs
):
    grads, refs = refs[:quarters], refs[quarters:]
    *kv_refs, dq_ref, keep_ref, send_ref, grad_ref = refs
    size = grads[0].shape[0]
    for k, ref in enumerate(grads):
        index = lax.rem(place_ref[4] + k, quarters)
        grad_ref[pl.ds(pl.multiple_of(index * size, size), size)] = ref[...]
    kv = whole_of(kv_refs)
    narrow = kv.shape[1] // 2
    bias = jnp.where(all_ref[...] <= own_ref[...], 0.0, -1e30)
    d_queries, d_keys, d_values = [], [], []
    for pair in range(heads // group):
        kv_at = pair * HEAD_SIZE
        key = kv[:, kv_at : kv_at + HEAD_SIZE]
        value = kv[:, narrow + kv_at : narrow + kv_at + HEAD_SIZE]
        d_key, d_value = 0.0, 0.0
        for h in range(pair * group, (pair + 1) * group):
            at = h * HEAD_SIZE
            query, grad = q_ref[:, at : at + HEAD_SIZE], grad_ref[:, at : at + HEAD_SIZE]
            probs = jnp.exp(nt(query, key) + bias - lse_ref[:, h : h + 1])
            d_probs = nt(grad, value)
            delta = jnp.sum(probs * d_probs, axis=1, keepdims=True)
            d_scores = (probs * (d_probs - delta)).astype(BF16)
            d_queries.append(nn(d_scores, key) * ATTN_MULT)
            d_key = d_key + tn(d_scores, query)
            d_value = d_value + tn(probs.astype(BF16), grad)
        d_keys.append(d_key)
        d_values.append(d_value)
    d_kv = jnp.concatenate(d_keys + d_values, axis=1).astype(BF16)
    rows = d_kv.shape[0] // blocks
    for m in range(blocks):
        ref = (keep_ref, send_ref)[m % 2]
        ref[m // 2 * rows : (m // 2 + 1) * rows] = d_kv[m * rows : (m + 1) * rows]
    d_query = jnp.concatenate(d_queries, axis=1)
    dq_ref[...] = rotate(d_query, cos_ref[...], -sin_ref[...]).astype(BF16)


def attend_back(blocks, query, kv, own_places, all_places, lse, grads, place, cosine, sine, heads, group):
    return call(
        functools.partial(attend_back_kernel, heads, group, len(grads), blocks),
        (shape(query.shape, BF16),)
        + (shape((sum(b.shape[0] for b in kv) // 2, kv[0].shape[1]), BF16),) * 2,
        (query, own_places, all_places, lse, cosine, sine, *grads, *kv),
        "attend_back",
        smem=(place,),
        scratch_shapes=[pltpu.VMEM(query.shape, BF16)],
    )


def gate_columns(gates, base, pair, units):
    lane = lax.broadcasted_iota(jnp.int32, gates.shape, 1)
    columns = [
        jnp.sum(jnp.where(lane == base + i, gates, 0.0), axis=1, keepdims=True) for i in range(pair)
    ]
    return jnp.concatenate(
        [jnp.broadcast_to(column, (gates.shape[0], units)) for column in columns], axis=1
    )


def whole_weight(first, own_ref, other_refs):
    pair = own_ref.shape[0]
    own = jnp.concatenate([own_ref[i] for i in range(pair)], axis=1)
    if not other_refs:
        return own
    other = jnp.concatenate([other_refs[0][i] for i in range(pair)], axis=1)
    for at, ref in enumerate(other_refs[1:], 1):
        here = jnp.concatenate([ref[i] for i in range(pair)], axis=1)
        other = jnp.where(pl.program_id(0) == at, here, other)
    return jnp.concatenate([jnp.where(first, own, other), jnp.where(first, other, own)], axis=0)


def experts_kernel(blocks, sources, counts, width, place_ref, router_ref, *refs):
    x_refs, g_refs, refs = refs[:sources], refs[sources : 2 * sources], refs[2 * sources :]
    (wg0_ref, wu0_ref, wd0_ref), refs = refs[:3], refs[3:]
    wg1_refs, refs = refs[: counts[0]], refs[counts[0] :]
    wu1_refs, refs = refs[: counts[1]], refs[counts[1] :]
    wd1_refs, refs = refs[: counts[2]], refs[counts[2] :]
    keep_ref, send_ref, own_ref, h_ref, dg_ref, du_ref, *refs = refs
    x_ref, grad_ref, gates_ref, din_acc, dgates_acc = refs
    step, steps = pl.program_id(0), pl.num_programs(0)
    pair, _, units = wg0_ref.shape
    first = place_ref[0] == 0
    base = place_ref[1] + step * pair
    rows = x_ref.shape[0] // blocks

    @pl.when(step == 0)
    def _():
        rows_in = whole_of(x_refs)
        x_ref[...] = rows_in
        grad_ref[...] = whole_of(g_refs)
        mask = grad_ref[:, width:].astype(F32)
        logits = jnp.where(mask > 0, nn(rows_in, router_ref[...]), -1e30)
        gates = mask * jnp.exp(logits - jnp.max(logits, axis=1, keepdims=True))
        gates = gates / jnp.sum(gates, axis=1, keepdims=True)
        gates_ref[...] = gates
        own_ref[...] = gates

    rows_in, rows_grad, gates = x_ref[...], grad_ref[:, :width], gates_ref[...]
    w_gate = whole_weight(first, wg0_ref, wg1_refs)
    w_up = whole_weight(first, wu0_ref, wu1_refs)
    w_down = whole_weight(first, wd0_ref, wd1_refs)
    wide = gate_columns(gates, base, pair, units)
    gate_pre, up_pre = nn(rows_in, w_gate), nn(rows_in, w_up)
    sigma = 0.5 * jnp.tanh(0.5 * gate_pre) + 0.5
    silu_gate = gate_pre * sigma
    active = silu_gate * up_pre
    h_ref[...] = (wide * active).astype(BF16)
    raw = nn(rows_grad, w_down)
    product = raw * active
    lane = lax.broadcasted_iota(jnp.int32, gates.shape, 1)
    d_gates = jnp.zeros_like(gates)
    for i in range(pair):
        column = RESID_MULT * jnp.sum(product[:, i * units : (i + 1) * units], axis=1, keepdims=True)
        d_gates = jnp.where(lane == base + i, column, d_gates)
    d_active = (RESID_MULT * wide) * raw
    d_gate_pre = (d_active * up_pre * sigma * (1.0 + gate_pre * (1.0 - sigma))).astype(BF16)
    d_up_pre = (d_active * silu_gate).astype(BF16)
    dg_ref[...], du_ref[...] = d_gate_pre, d_up_pre
    d_in = nt(d_gate_pre, w_gate) + nt(d_up_pre, w_up)

    @pl.when(step == 0)
    def _():
        din_acc[...] = d_in
        dgates_acc[...] = d_gates

    @pl.when(step > 0)
    def _():
        din_acc[...] += d_in
        dgates_acc[...] += d_gates

    @pl.when(step == steps - 1)
    def _():
        for m in range(blocks):
            ref = (keep_ref, send_ref)[m % 2]
            to, at = slice(m // 2 * rows, (m // 2 + 1) * rows), slice(m * rows, (m + 1) * rows)
            ref[to, :width] = din_acc[at].astype(BF16)
            ref[to, width:] = split_lanes(dgates_acc[at])


def held(a):
    return pl.BlockSpec(a.shape, lambda i: (0,) * len(a.shape))


def run_experts(blocks, chunks, x_blocks, g_blocks, router, place, weights, others):
    tokens, lanes = sum(b.shape[0] for b in x_blocks), g_blocks[0].shape[1]
    width = x_blocks[0].shape[1]
    count, _, units = weights[0].shape
    pair = count // chunks
    moving = lambda w: pl.BlockSpec((pair, w.shape[1], units), lambda i: (i, 0, 0))
    column = pl.BlockSpec((tokens, pair * units), lambda i: (0, i))
    outs = (
        [shape((tokens // 2, lanes), BF16)] * 2
        + [shape((tokens, LANES), F32)]
        + [shape((tokens, count * units), BF16)] * 3
    )
    flat = sum(others, [])
    return pl.pallas_call(
        functools.partial(experts_kernel, blocks, len(x_blocks), [len(o) for o in others], width),
        grid=(chunks,),
        out_shape=tuple(outs),
        in_specs=[pl.BlockSpec(memory_space=pltpu.SMEM), held(router)]
        + [held(b) for b in x_blocks + g_blocks]
        + [moving(w) for w in weights]
        + [held(o) for o in flat],
        out_specs=tuple(held(o) for o in outs[:3]) + (column,) * 3,
        scratch_shapes=[
            pltpu.VMEM((tokens, width), BF16),
            pltpu.VMEM((tokens, lanes), BF16),
            pltpu.VMEM((tokens, LANES), F32),
            pltpu.VMEM((tokens, width), F32),
            pltpu.VMEM((tokens, LANES), F32),
        ],
        compiler_params=pltpu.CompilerParams(vmem_limit_bytes=VMEM_BYTES),
        name="experts",
    )(place, router, *x_blocks, *g_blocks, *weights, *flat)


def grads_kernel(sources, parts, width, place_ref, *refs):
    x_refs, g_refs, refs = refs[:sources], refs[sources : 2 * sources], refs[2 * sources :]
    h_refs, dg_refs, du_refs = (refs[i * parts : (i + 1) * parts] for i in range(3))
    grad_refs = refs[3 * parts :]
    pair, half, units = grad_refs[0].shape
    first = place_ref[0] == 0

    def halves(grad, own_ref, other_ref):
        own = jnp.where(first, grad[:half], grad[half:]).astype(BF16)
        other = jnp.where(first, grad[half:], grad[:half]).astype(BF16)
        for i in range(pair):
            own_ref[i] = own[:, i * units : (i + 1) * units]
            other_ref[i] = other[:, i * units : (i + 1) * units]

    rows_in, rows_grad = whole_of(x_refs), whole_of(g_refs)[:, :width]
    halves(RESID_MULT * tn(rows_grad, whole_of(h_refs)), grad_refs[4], grad_refs[5])
    halves(tn(rows_in, whole_of(dg_refs)), grad_refs[0], grad_refs[1])
    halves(tn(rows_in, whole_of(du_refs)), grad_refs[2], grad_refs[3])


def run_grads(x_blocks, g_blocks, place, hidden, d_gate, d_up, dims, chunks):
    parts, tokens = len(hidden), sum(b.shape[0] for b in x_blocks)
    count, half, units = dims
    pair = count // chunks
    width = x_blocks[0].shape[1]
    moving = pl.BlockSpec((pair, half, units), lambda i: (i, 0, 0))
    column = pl.BlockSpec((tokens // parts, pair * units), lambda i: (0, i))
    return pl.pallas_call(
        functools.partial(grads_kernel, len(x_blocks), parts, width),
        grid=(chunks,),
        out_shape=(shape(dims, BF16),) * 6,
        in_specs=[pl.BlockSpec(memory_space=pltpu.SMEM)]
        + [held(b) for b in x_blocks + g_blocks]
        + [column] * (3 * parts),
        out_specs=(moving,) * 6,
        compiler_params=pltpu.CompilerParams(vmem_limit_bytes=VMEM_BYTES),
        name="grads",
    )(place, *x_blocks, *g_blocks, *hidden, *d_gate, *d_up)


def outputs_kernel(blocks, chunks, place_ref, h_ref, wd0_ref, *refs):
    wd1_refs, out_refs, out_acc = refs[:chunks], refs[chunks:-1], refs[-1]
    step, steps = pl.program_id(0), pl.num_programs(0)
    out = nt(h_ref[...], whole_weight(place_ref[0] == 0, wd0_ref, wd1_refs))

    @pl.when(step == 0)
    def _():
        out_acc[...] = out

    @pl.when(step > 0)
    def _():
        out_acc[...] += out

    @pl.when(step == steps - 1)
    def _():
        rows = out_acc.shape[0] // blocks
        for m in range(blocks):
            to = slice(m // 2 * rows, (m // 2 + 1) * rows)
            out_refs[m % 2][to] = out_acc[m * rows : (m + 1) * rows].astype(BF16)


def run_outputs(blocks, place, hidden, w_own, others):
    chunks = len(others)
    count, half, units = w_own.shape
    pair, tokens, width = count // chunks, hidden.shape[0], 2 * half
    outs = (shape((tokens // 2, width), BF16),) * 2
    return pl.pallas_call(
        functools.partial(outputs_kernel, blocks, chunks),
        grid=(chunks,),
        out_shape=outs,
        in_specs=[
            pl.BlockSpec(memory_space=pltpu.SMEM),
            pl.BlockSpec((tokens, pair * units), lambda i: (0, i)),
            pl.BlockSpec((pair, half, units), lambda i: (i, 0, 0)),
        ]
        + [held(o) for o in others],
        out_specs=tuple(held(o) for o in outs),
        scratch_shapes=[pltpu.VMEM((tokens, width), F32)],
        compiler_params=pltpu.CompilerParams(vmem_limit_bytes=VMEM_BYTES),
        name="outputs",
    )(place, hidden, w_own, *others)


def rms_back(rows, gain, grad):
    scale = lax.rsqrt(jnp.mean(rows * rows, axis=-1, keepdims=True) + NORM_EPS)
    d_gain = jnp.sum(grad * rows * scale, axis=0, keepdims=True)
    pulled = grad * gain
    mean = jnp.mean(pulled * rows, axis=-1, keepdims=True)
    return scale * pulled - rows * (scale * scale * scale) * mean, d_gain


def body(
    hidden_in,
    positions,
    routes,
    out_grad,
    attn_gain,
    query_weight,
    key_matrix,
    value_matrix,
    out_weight,
    moe_gain,
    router_weight,
    gate_weight,
    up_weight,
    down_weight,
):
    shards, contexts, tensors = (lax.axis_size(a) for a in ("shards", "context", "tensor"))
    shard, context, tensor = (lax.axis_index(a) for a in ("shards", "context", "tensor"))
    owners = shards * contexts
    steps = stepped()
    owner = shard * contexts + context if steps else 0 * shard
    flip = context if steps else 0 * context
    rows, width = hidden_in.shape[1:]
    chunk, quarter = width // owners, rows // tensors
    wide, narrow = query_weight.shape[1], key_matrix.shape[1]
    heads, group = wide // HEAD_SIZE, wide // narrow
    expert_count, local_experts = router_weight.shape[1], gate_weight.shape[0]
    columns = 2 * wide + 2 * narrow
    gates_at = tensor if steps else context * tensors + tensor
    place = jnp.stack([shard, context * local_experts, flip, owner, tensor, gates_at])
    place = place.astype(jnp.int32)

    packed = jnp.concatenate(
        [
            jnp.concatenate([query_weight, key_matrix, value_matrix, out_weight], axis=1),
            jnp.pad(
                jnp.concatenate([attn_gain, moe_gain])[None], ((0, 7), (0, columns - 2 * chunk))
            ),
            jnp.pad(
                router_weight.reshape(8, chunk * expert_count // 8),
                ((0, 0), (0, columns - chunk * expert_count // 8)),
            ),
        ],
        axis=0,
    )
    grad_rows = out_grad[0]
    names = jnp.arange(LANES, dtype=jnp.int32)
    mask = jnp.any(routes[0][:, :, None] == names[None, None, :], axis=1).astype(BF16)
    gathered = gather_owners(packed)
    if steps:
        even, odd = gathered[:4], gathered[4:]
        pieces = [p for pair in zip(even, odd) for p in pair]
        gain_a = jnp.concatenate([p[chunk : chunk + 1, :chunk] for p in pieces], axis=1).astype(F32)
    else:
        stack = gathered[0]
        pieces = [stack[:, :chunk].reshape(width, columns)]
        gain_a = stack[:, chunk, :chunk].reshape(1, width).astype(F32)

    chunks = 2 if local_experts % 2 == 0 else 1
    size = local_experts // chunks
    weights = [lax.all_gather(w, "shards", axis=1, tiled=True) for w in (gate_weight, up_weight)]
    weights.append(down_weight)
    down_other = [swap(down_weight[i * size : (i + 1) * size], "shards", 1) for i in range(chunks)]
    others = [[], [], down_other]

    place_all = positions[0].reshape(contexts, rows)
    own_places = cut(place_all, context, 1).reshape(rows, 1)
    if steps:
        place_all = jnp.concatenate(xor_blocks([place_all[i] for i in range(contexts)], context))
    all_places = place_all.reshape(1, contexts * rows)
    half = HEAD_SIZE // 2
    frequency = ROPE_BASE ** (-2.0 * jnp.arange(half, dtype=F32) / HEAD_SIZE)
    angles = own_places.astype(F32) * frequency[None, :]
    cosine, sine = jnp.cos(angles), jnp.sin(angles)
    cosine = jnp.concatenate([cosine] * 4, axis=1)
    sine = jnp.concatenate([-sine, sine] * 2, axis=1)

    hidden = hidden_in[0]
    hidden_rel = hidden
    if steps:
        hidden_rel = jnp.concatenate(xor_blocks(columns_of(hidden, owners), owner), axis=1)
    normed_a, query, kv, w_qkv = project(
        hidden_rel, gain_a, pieces, cosine, sine, wide, narrow, chunk if steps else width
    )
    kv_all = gather_context(kv)
    attended, lse = attend(query, kv_all, own_places, all_places, heads, group)

    if steps:
        evens = jnp.concatenate([p[:chunk, columns - wide :] for p in even], axis=0)
        evens = [evens] + [turn(evens, k) for k in range(1, tensors)]
        w_out = call(
            functools.partial(assemble_kernel, (0, 2, 4, 6, 1, 3, 5, 7), chunk),
            [shape((width, wide * tensors), BF16)],
            (swap(jnp.concatenate(evens, axis=0), "context", 1), *evens),
            "assemble",
            smem=(place,),
        )[0]
        late = [after(p, query) for p in pieces]
        gain_m = [p[chunk : chunk + 1, chunk : 2 * chunk] for p in late]
        gain_m = jnp.concatenate(xor_blocks(gain_m, owner), axis=1).astype(F32)
        router = [p[chunk + 8 : chunk + 16, : chunk * expert_count // 8] for p in late]
        router = jnp.concatenate(xor_blocks(router, owner), axis=0).reshape(width, expert_count)
    else:
        own = pieces[0][:, columns - wide :]
        w_out = jnp.concatenate([own] + [turn(own, k) for k in range(1, tensors)], axis=1)
        gain_m = stack[:, chunk, chunk : 2 * chunk].reshape(1, width).astype(F32)
        router = stack[:, chunk + 8 :, : chunk * expert_count // 8].reshape(width, expert_count)
    router = jnp.pad(router, ((0, 0), (0, LANES - expert_count)))
    attended = after(attended, down_other[0])
    attended_all = [attended] + [turn(attended, k) for k in range(1, tensors)]
    middle, normed_m = call(
        middle_kernel,
        (shape(hidden.shape, F32), shape(hidden.shape, BF16)),
        (hidden, gain_m, w_out, *attended_all),
        "middle",
    )

    x_blocks = gather_context(normed_m)
    g_blocks = gather_context(jnp.concatenate([grad_rows, mask], axis=1))
    if steps:
        parts = [(x_blocks[:2], g_blocks[:2]), (x_blocks[2:], g_blocks[2:])]
    else:
        parts = [
            ([cut(x_blocks[0], i, PART_ROWS)], [cut(g_blocks[0], i, PART_ROWS)])
            for i in range(contexts * rows // PART_ROWS)
        ]
    found = [run_experts(2, chunks, xs, gs, router, place, weights, others) for xs, gs in parts]
    gates = found[0][2] if steps else jnp.concatenate([f[2] for f in found], axis=0)

    def to_quarters(kept, sent):
        if steps:
            core = [swap(b, "context", 1) for b in sent]
            send = fold((kept[1], core[1]), place, width, 0)[0]
            return send, fold((kept[0], core[0], swap(send, "context", 2)), place, width, tensors)
        whole = jnp.concatenate([b for pair in zip(kept, sent) for b in pair], axis=0)
        own = lax.psum_scatter(whole, "context", scatter_dimension=0, tiled=True)
        return own, fold((own,), place, width, tensors)

    early, d_normed = to_quarters([f[0] for f in found], [f[1] for f in found])
    outputs = [
        run_outputs(2, place, after(f[3], d_normed[0]), down_weight, down_other) for f in found
    ]
    dims = gate_weight.shape
    if steps:
        columns_in = [[f[i] for f in found] for i in (3, 4, 5)]
        columns_in[0][0] = after(columns_in[0][0], early)
        grads = run_grads(x_blocks, g_blocks, place, *columns_in, dims, chunks)
    else:
        grads = [
            run_grads(xs, gs, place, [f[3]], [f[4]], [f[5]], dims, chunks)
            for f, (xs, gs) in zip(found, parts)
        ]
        grads = [sum(g.astype(F32) for g in one).astype(BF16) for one in zip(*grads)]

    parts = [d_normed[0]] + [turn(d_normed[k], k) for k in range(1, tensors)]
    middle_q = cut(middle, tensor, quarter)
    outs = (
        shape((quarter, width), F32),
        shape((quarter, width), BF16),
        shape((1, width), F32),
        shape((width, LANES), F32),
    ) + (shape((quarter, wide), BF16),) * tensors
    own = lambda lanes: pl.BlockSpec((quarter, lanes), lambda i, at: (at[4], 0))
    gates_own = pl.BlockSpec((quarter, LANES), lambda i, at: (at[5], 0))
    full = lambda a: pl.BlockSpec(a.shape, lambda i, at: (0, 0))
    d_middle, d_attn, d_gain_m, d_router, *d_attended = pl.pallas_call(
        functools.partial(middle_back_kernel, width),
        out_shape=outs,
        grid_spec=pltpu.PrefetchScalarGridSpec(
            num_scalar_prefetch=1,
            grid=(1,),
            in_specs=[own(width), own(width), full(gain_m), own(width), gates_own, full(router), full(w_out)]
            + [full(p) for p in parts],
            out_specs=tuple(full(o) for o in outs),
        ),
        compiler_params=pltpu.CompilerParams(vmem_limit_bytes=VMEM_BYTES),
        name="middle_back",
    )(place, middle, normed_m, gain_m, grad_rows, after(gates, outputs[0][0]), router, w_out, *parts)

    came = [swap(g, "shards", 1) for g in (grads[5], grads[1], grads[3])]

    d_attended = [turn(d, -k) if k else d for k, d in enumerate(d_attended)]
    out_early, moe_out = to_quarters(*([after(o[i], d_attn) for o in outputs] for i in range(2)))
    d_query, d_kv, d_kv_send = attend_back(
        contexts if steps else 2,
        after(query, came[0], out_early),
        kv_all,
        own_places,
        all_places,
        lse,
        d_attended,
        place,
        cosine,
        sine,
        heads,
        group,
    )
    if steps:
        d_kv = d_kv.astype(F32) + swap(d_kv_send, "context", 1).astype(F32)
        d_kv, d_kv_send = d_kv[:rows], swap(d_kv[rows:].astype(BF16), "context", 2)
    else:
        d_kv = jnp.concatenate([d_kv, d_kv_send], axis=0)
        d_kv = lax.psum_scatter(d_kv, "context", scatter_dimension=0, tiled=True)
        d_kv_send = jnp.zeros_like(d_kv)
    *d_normed, d_lin = call(
        functools.partial(project_back_kernel, narrow),
        [shape((quarter, width), F32)]
        + [shape((quarter, width), BF16)] * (tensors - 1)
        + [shape((rows, wide + 2 * narrow), BF16)],
        (after(d_query, came[1], moe_out[0]), d_kv, d_kv_send, cosine[:, :narrow], sine[:, :narrow], w_qkv),
        "project_back",
        smem=(place,),
        scratch_shapes=[pltpu.VMEM((rows, width), F32)],
    )
    parts = [turn(d_normed[k], k) for k in range(1, tensors)]
    d_attn = gather_tensor(after(d_attn, d_kv))
    if steps:
        kept, sent = call(
            functools.partial(weights_back_kernel, OWNER_ORDER, chunk),
            [shape((width // 2, columns), BF16)] * 2,
            (normed_a, d_lin, d_attn, attended),
            "weights_back",
            smem=(place,),
            scratch_shapes=[pltpu.VMEM((width, wide), F32)],
        )
        tie, d_weights = scatter_owners(kept, sent, BF16)
        parts[0] = after(parts[0], tie)
    d_normed = d_normed[0] + sum(p.astype(F32) for p in parts)
    d_rows, d_gain_a = rms_back(
        cut(hidden_rel, tensor, quarter).astype(F32), gain_a, d_normed
    )
    if steps:
        d_rows = jnp.concatenate(xor_blocks(columns_of(d_rows, owners), owner), axis=1)
    in_grad = gather_tensor((d_middle + d_rows).astype(BF16)).astype(F32)

    moe_out = moe_out[0] + sum(turn(moe_out[k], k).astype(F32) for k in range(1, tensors))
    block_out = gather_tensor((middle_q + RESID_MULT * moe_out).astype(BF16))

    expert_grads = [
        own.astype(F32) + other.astype(F32)
        for own, other in ((grads[0], came[1]), (grads[2], came[2]), (grads[4], came[0]))
    ]
    small = jnp.concatenate([d_gain_m, d_router[:, :expert_count].T], axis=0)
    if steps:
        small = xor_blocks(columns_of(small, owners), owner)
        small = [
            jnp.concatenate([a, b], axis=0) for a, b in zip(columns_of(d_gain_a, owners), small)
        ]
        small = [jnp.pad(b, ((0, -b.shape[0] % 8), (0, 0))) for b in small]
        kept, sent = (
            jnp.concatenate([small[r] for r in OWNER_ORDER[i : i + 4]], axis=0) for i in (0, 4)
        )
        small = scatter_owners(kept, sent, F32)[1]
    else:
        over = ("shards", "context")
        d_weights = jnp.concatenate([tn(normed_a, d_lin), tn(d_attn, attended)], axis=1)
        d_weights = lax.psum_scatter(
            d_weights.astype(BF16), over, scatter_dimension=0, tiled=True
        ).astype(F32)
        small = jnp.concatenate([d_gain_a, small], axis=0)
        small = jnp.swapaxes(small.reshape(-1, owners, chunk), 0, 1)
        small = lax.psum_scatter(small, over, scatter_dimension=0)
    small = butterfly(small)
    return (
        block_out[None],
        in_grad[None],
        small[0],
        d_weights[:, :wide],
        d_weights[:, wide : wide + narrow],
        d_weights[:, wide + narrow : wide + 2 * narrow],
        d_weights[:, wide + 2 * narrow :],
        small[1],
        small[2 : 2 + expert_count].T,
        expert_grads[0],
        expert_grads[1],
        expert_grads[2],
    )


def solution(mesh):
    owned = ("shards", "context")
    rows = P("shards", "context", None)
    split = P(owned, "tensor")
    expert = P("context", "shards", "tensor")
    return jax.shard_map(
        body,
        mesh=mesh,
        in_specs=(
            rows,
            P("shards", None),
            rows,
            rows,
            P(owned),
            split,
            split,
            split,
            split,
            P(owned),
            P(owned, None),
            expert,
            expert,
            expert,
        ),
        out_specs=(
            rows,
            rows,
            P(owned),
            split,
            split,
            split,
            split,
            P(owned),
            P(owned, None),
            expert,
            expert,
            expert,
        ),
        check_vma=False,
    )
```

```python
import functools

import jax
import jax.numpy as jnp
from jax import lax
from jax.experimental import pallas as pl
from jax.experimental.pallas import tpu as pltpu
from jax.sharding import PartitionSpec as P

HEAD_SIZE = 64
NORM_EPS = 1e-06
ATTN_MULT = 0.015625
RESID_MULT = 0.22
ROPE_BASE = 10000.0
F32 = jnp.float32
BF16 = jnp.bfloat16
VMEM_BYTES = 56 * 1024 * 1024
PART_ROWS = 1024
MICROSECONDS = {
    "project": 3,
    "assemble": 3,
    "middle": 4,
    "fold": 2.5,
    "middle_back": 4.5,
    "project_back": 3,
    "weights_back": 3,
    "attend": 4,
    "attend_back": 6,
    "experts": 12,
    "grads": 12,
    "outputs": 9,
}
LANES = 128


def swap(x, axis, bit):
    devices = lax.axis_size(axis)
    return lax.ppermute(x, axis, [(i, i ^ bit) for i in range(devices)])


def turn(x, k):
    return swap(x, "tensor", k)


def stepped():
    return lax.axis_size("context") == 4 and lax.axis_size("shards") == 2


def after(x, *others):
    return lax.optimization_barrier((x,) + others)[0]


def gather_context(x):
    if not stepped():
        return [lax.all_gather(x, "context", axis=0, tiled=True)]
    across = swap(x, "context", 2)
    return [x, swap(x, "context", 1), across, swap(across, "context", 1)]


def swap_tensor(x, bit):
    return swap(x, "tensor", bit)


def gather_owners(x):
    if not stepped():
        return [lax.all_gather(x, ("shards", "context"))]
    far = []
    for m in (2, 4, 6):
        far.append(lax.ppermute(x, ("shards", "context"), [(i, i ^ m) for i in range(8)]))
    near = swap(x, "context", 1)
    odd = swap(jnp.concatenate(far, axis=0), "context", 1)
    size = x.shape[0]
    return [x] + far + [near] + [odd[i * size : (i + 1) * size] for i in range(3)]


OWNER_ORDER = (0, 4, 2, 6, 1, 5, 3, 7)


def scatter_owners(keep, send, travel):
    size = keep.shape[0] // 4
    total = keep.astype(F32) + swap(send.astype(travel), "context", 1).astype(F32)
    far = swap(total[2 * size :].astype(travel), "context", 2).astype(F32)
    total = total[: 2 * size] + far
    return total, total[:size] + swap(total[size:].astype(travel), "shards", 1).astype(F32)


def butterfly(x):
    bit = 1
    while bit < lax.axis_size("tensor"):
        x = x + lax.ppermute(x, "tensor", [(i, i ^ bit) for i in range(lax.axis_size("tensor"))])
        bit *= 2
    return x


def xor_blocks(pieces, index):
    pieces, bit = list(pieces), 1
    while bit < len(pieces):
        flag = (index & bit) != 0
        pieces = [jnp.where(flag, pieces[i ^ bit], pieces[i]) for i in range(len(pieces))]
        bit *= 2
    return pieces


def columns_of(x, count):
    size = x.shape[1] // count
    return [x[:, i * size : (i + 1) * size] for i in range(count)]


def cut(x, index, size):
    return lax.dynamic_slice_in_dim(x, index * size, size, axis=0)


def gather_tensor(x):
    devices, me = lax.axis_size("tensor"), lax.axis_index("tensor")
    size = x.shape[0]
    whole = jnp.zeros((size * devices,) + x.shape[1:], x.dtype)
    for k in range(devices):
        piece = turn(x, k) if k else x
        whole = lax.dynamic_update_slice_in_dim(whole, piece, (me ^ k) * size, axis=0)
    return whole


def nn(a, b):
    return lax.dot_general(a, b, (((1,), (0,)), ((), ())), preferred_element_type=F32)


def tn(a, b):
    return lax.dot_general(a, b, (((0,), (0,)), ((), ())), preferred_element_type=F32)


def nt(a, b):
    return lax.dot_general(a, b, (((1,), (1,)), ((), ())), preferred_element_type=F32)


def vmem():
    return pl.BlockSpec(memory_space=pltpu.VMEM)


def rotate(x, cosine, sine):
    lanes = x.shape[1]
    times = lanes // cosine.shape[1]
    lane = lax.broadcasted_iota(jnp.int32, x.shape, 1)
    half = HEAD_SIZE // 2
    partner = jnp.where(
        lane % HEAD_SIZE < half, pltpu.roll(x, lanes - half, 1), pltpu.roll(x, half, 1)
    )
    return x * jnp.concatenate([cosine] * times, 1) + partner * jnp.concatenate([sine] * times, 1)


def cost(name):
    flops = int(MICROSECONDS[name] * 1.15e9)
    return pl.CostEstimate(flops=flops, transcendentals=0, bytes_accessed=0)


def call(kernel, out_shape, operands, name, smem=(), **more):
    specs = [pl.BlockSpec(memory_space=pltpu.SMEM)] * len(smem) + [vmem()] * len(operands)
    return pl.pallas_call(
        kernel,
        out_shape=tuple(out_shape),
        in_specs=specs,
        out_specs=(vmem(),) * len(out_shape),
        compiler_params=pltpu.CompilerParams(vmem_limit_bytes=VMEM_BYTES),
        cost_estimate=cost(name),
        name=name,
        **more,
    )(*smem, *operands)


def shape(dims, dtype):
    return jax.ShapeDtypeStruct(tuple(dims), dtype)


def project_kernel(wide, narrow, chunk, hid_ref, gain_ref, cos_ref, sin_ref, *refs):
    *pieces, norm_ref, q_ref, kv_ref, w_ref = refs
    for i, piece in enumerate(pieces):
        w_ref[i * chunk : (i + 1) * chunk] = piece[:chunk, : w_ref.shape[1]]
    hid = hid_ref[...].astype(F32)
    scale = lax.rsqrt(jnp.mean(hid * hid, axis=1, keepdims=True) + NORM_EPS)
    normed = (hid * scale * gain_ref[...]).astype(BF16)
    norm_ref[...] = normed
    lin = nn(normed, w_ref[...])
    turned = rotate(lin[:, : wide + narrow], cos_ref[...], sin_ref[...]).astype(BF16)
    q_ref[...] = turned[:, :wide] * ATTN_MULT
    kv_ref[:, :narrow] = turned[:, wide:]
    kv_ref[:, narrow:] = lin[:, wide + narrow :].astype(BF16)


def project(hidden, gain, pieces, cosine, sine, wide, narrow, chunk):
    rows, width = hidden.shape
    return call(
        functools.partial(project_kernel, wide, narrow, chunk),
        (
            shape((rows, width), BF16),
            shape((rows, wide), BF16),
            shape((rows, 2 * narrow), BF16),
            shape((width, wide + 2 * narrow), BF16),
        ),
        (hidden, gain, cosine, sine, *pieces),
        "project",
    )


def assemble_kernel(order, chunk, place_ref, even_ref, odd_ref, out_ref):
    wide = even_ref.shape[1]
    size = len(order) // 2 * chunk
    for k in range(even_ref.shape[0] // size):
        for at, r in enumerate(order):
            start = k * size + at % (len(order) // 2) * chunk
            rows = pl.ds(pl.multiple_of((place_ref[3] ^ r) * chunk, chunk), chunk)
            source = (even_ref, odd_ref)[r % 2]
            out_ref[rows, k * wide : (k + 1) * wide] = source[start : start + chunk]


def middle_kernel(hid_ref, gain_ref, w_ref, *refs):
    *att_refs, mid_ref, norm_ref = refs
    attended = jnp.concatenate([r[...] for r in att_refs], axis=1)
    middle = hid_ref[...].astype(F32) + RESID_MULT * nt(attended, w_ref[...])
    scale = lax.rsqrt(jnp.mean(middle * middle, axis=1, keepdims=True) + NORM_EPS)
    mid_ref[...] = middle
    norm_ref[...] = (middle * scale * gain_ref[...]).astype(BF16)


def split_lanes(x):
    high = x.astype(BF16)
    low = (x - high.astype(F32)).astype(BF16).astype(F32)
    return (high.astype(F32) + pltpu.roll(low, LANES // 2, 1)).astype(BF16)


def join_lanes(x):
    lane = lax.broadcasted_iota(jnp.int32, x.shape, 1)
    return jnp.where(lane < LANES // 2, x + pltpu.roll(x, LANES // 2, 1), 0.0)


def fold_kernel(width, quarters, terms, place_ref, *refs):
    total = refs[0][...].astype(F32)
    for ref in refs[1:terms]:
        total = total + ref[...].astype(F32)
    if not quarters:
        ref = refs[terms]
        ref[:, :width] = total[:, :width].astype(BF16)
        if total.shape[1] > width:
            ref[:, width:] = split_lanes(join_lanes(total[:, width:]))
        return
    own_ref, *send_refs, total_ref = refs[terms:]
    if total.shape[1] > width:
        total = jnp.concatenate([total[:, :width], join_lanes(total[:, width:])], axis=1)
    total_ref[...] = total
    size = own_ref.shape[0]

    def part(index):
        index = place_ref[4] ^ index
        return total_ref[pl.ds(pl.multiple_of(index * size, size), size)]

    own_ref[...] = part(0)
    for k, ref in enumerate(send_refs, 1):
        found = part(k)
        ref[:, :width] = found[:, :width].astype(BF16)
        if found.shape[1] > width:
            ref[:, width:] = split_lanes(found[:, width:])


def fold(terms, place, width, quarters):
    rows, lanes = terms[0].shape
    size = rows // max(quarters, 1)
    outs = [shape((size, lanes), BF16)]
    if quarters:
        outs = [shape((size, lanes), F32)] + outs * (quarters - 1)
    return call(
        functools.partial(fold_kernel, width, quarters, len(terms)),
        outs,
        terms,
        "fold",
        smem=(place,),
        scratch_shapes=[pltpu.VMEM((rows, lanes), F32)] if quarters else [],
    )


def middle_back_kernel(width, _place_ref, mid_ref, norm_ref, gain_ref, grad_ref, gates_ref, router_ref, w_ref, *refs):
    outs = (len(refs) - 4) // 2
    parts, refs = refs[:outs], refs[outs:]
    dmid_ref, dattn_ref, dgain_ref, drouter_ref = refs[:4]
    total = parts[0][...]
    for part in parts[1:]:
        total = total + part[...].astype(F32)
    gates, d_gates = gates_ref[...], join_lanes(total[:, width:])
    d_picked = gates * (d_gates - jnp.sum(gates * d_gates, axis=1, keepdims=True))
    d_logits = d_picked.astype(BF16)
    drouter_ref[...] = tn(norm_ref[...], d_logits)
    d_normed = total[:, :width] + nt(d_logits, router_ref[...])
    d_rows, d_gain = rms_back(mid_ref[...], gain_ref[...], d_normed)
    d_middle = grad_ref[...].astype(F32) + d_rows
    d_attn = (RESID_MULT * d_middle).astype(BF16)
    dmid_ref[...], dattn_ref[...], dgain_ref[...] = d_middle, d_attn, d_gain
    d_attended = nn(d_attn, w_ref[...]).astype(BF16)
    wide = d_attended.shape[1] // outs
    for k, ref in enumerate(refs[4:]):
        ref[:, :wide] = d_attended[:, k * wide : (k + 1) * wide]
        if k:
            ref[:, wide:] = d_attn


def project_back_kernel(narrow, place_ref, dq_ref, keep_ref, came_ref, cos_ref, sin_ref, w_ref, hid_ref, *refs):
    own_ref, *send_refs, dlin_ref, dgain_ref, total_ref = refs
    d_kv = keep_ref[...].astype(F32) + came_ref[...].astype(F32)
    d_key = rotate(d_kv[:, :narrow], cos_ref[...], -sin_ref[...])
    d_lin = jnp.concatenate(
        [dq_ref[...], d_key.astype(BF16), d_kv[:, narrow:].astype(BF16)], axis=1
    )
    dlin_ref[...] = d_lin
    d_normed = nt(d_lin, w_ref[...])
    total_ref[...] = d_normed
    hid = hid_ref[...].astype(F32)
    scale = lax.rsqrt(jnp.mean(hid * hid, axis=1, keepdims=True) + NORM_EPS)
    dgain_ref[...] = jnp.sum(d_normed * hid * scale, axis=0, keepdims=True)
    size, quarters = own_ref.shape[0], 1 + len(send_refs)

    def part(k):
        index = place_ref[4] ^ k
        return total_ref[pl.ds(pl.multiple_of(index * size, size), size)]

    own_ref[...] = part(0)
    for k, ref in enumerate(send_refs, 1):
        ref[...] = part(k).astype(BF16)


def weights_back_kernel(order, chunk, place_ref, norm_ref, dlin_ref, att_ref, *refs):
    lin = tn(norm_ref[...], dlin_ref[...]).astype(BF16)
    *dattn_refs, keep_ref, send_ref, rows_ref, scratch_ref = refs
    size = dattn_refs[0].shape[0]
    for k, ref in enumerate(dattn_refs):
        columns = slice(ref.shape[1] - rows_ref.shape[1], None)
        rows_ref[pl.ds(pl.multiple_of((place_ref[4] ^ k) * size, size), size)] = ref[:, columns]
    scratch_ref[...] = tn(rows_ref[...], att_ref[...])
    split = lin.shape[1]
    for at, r in enumerate(order):
        ref = (keep_ref, send_ref)[r % 2]
        start = at % (len(order) // 2) * chunk
        rows = pl.ds(pl.multiple_of((place_ref[3] ^ r) * chunk, chunk), chunk)
        ref[start : start + chunk, :split] = lin[r * chunk : (r + 1) * chunk]
        ref[start : start + chunk, split:] = scratch_ref[rows].astype(BF16)


def whole_of(refs):
    return jnp.concatenate([r[...] for r in refs], axis=0) if len(refs) > 1 else refs[0][...]


def attend_kernel(heads, group, q_ref, own_ref, all_ref, *refs):
    *kv_refs, out_ref, lse_ref = refs
    kv = whole_of(kv_refs)
    narrow = kv.shape[1] // 2
    bias = jnp.where(all_ref[...] <= own_ref[...], 0.0, -1e30)
    for h in range(heads):
        at, kv_at = h * HEAD_SIZE, (h // group) * HEAD_SIZE
        key = kv[:, kv_at : kv_at + HEAD_SIZE]
        value = kv[:, narrow + kv_at : narrow + kv_at + HEAD_SIZE]
        scores = nt(q_ref[:, at : at + HEAD_SIZE], key) + bias
        top = jnp.max(scores, axis=1, keepdims=True)
        weights = jnp.exp(scores - top)
        total = jnp.sum(weights, axis=1, keepdims=True)
        out = nn(weights.astype(BF16), value) / total
        out_ref[:, at : at + HEAD_SIZE] = out.astype(BF16)
        lse_ref[:, h : h + 1] = top + jnp.log(total)


def attend(query, kv, own_places, all_places, heads, group):
    return call(
        functools.partial(attend_kernel, heads, group),
        (shape(query.shape, BF16), shape((query.shape[0], heads), F32)),
        (query, own_places, all_places, *kv),
        "attend",
    )


def attend_back_kernel(
    heads, group, quarters, blocks, place_ref, q_ref, own_ref, all_ref, lse_ref, cos_ref, sin_ref, *refs
):
    grads, refs = refs[:quarters], refs[quarters:]
    *kv_refs, dq_ref, keep_ref, send_ref, grad_ref = refs
    size = grads[0].shape[0]
    for k, ref in enumerate(grads):
        index = place_ref[4] ^ k
        grad_ref[pl.ds(pl.multiple_of(index * size, size), size)] = ref[:, : grad_ref.shape[1]]
    kv = whole_of(kv_refs)
    narrow = kv.shape[1] // 2
    bias = jnp.where(all_ref[...] <= own_ref[...], 0.0, -1e30)
    d_queries, d_keys, d_values = [], [], []
    for pair in range(heads // group):
        kv_at = pair * HEAD_SIZE
        key = kv[:, kv_at : kv_at + HEAD_SIZE]
        value = kv[:, narrow + kv_at : narrow + kv_at + HEAD_SIZE]
        d_key, d_value = 0.0, 0.0
        for h in range(pair * group, (pair + 1) * group):
            at = h * HEAD_SIZE
            query, grad = q_ref[:, at : at + HEAD_SIZE], grad_ref[:, at : at + HEAD_SIZE]
            probs = jnp.exp(nt(query, key) + bias - lse_ref[:, h : h + 1])
            d_probs = nt(grad, value)
            delta = jnp.sum(probs * d_probs, axis=1, keepdims=True)
            d_scores = (probs * (d_probs - delta)).astype(BF16)
            d_queries.append(nn(d_scores, key) * ATTN_MULT)
            d_key = d_key + tn(d_scores, query)
            d_value = d_value + tn(probs.astype(BF16), grad)
        d_keys.append(d_key)
        d_values.append(d_value)
    d_kv = jnp.concatenate(d_keys + d_values, axis=1).astype(BF16)
    rows = d_kv.shape[0] // blocks
    for m in range(blocks):
        ref = (keep_ref, send_ref)[m % 2]
        ref[m // 2 * rows : (m // 2 + 1) * rows] = d_kv[m * rows : (m + 1) * rows]
    d_query = jnp.concatenate(d_queries, axis=1)
    dq_ref[...] = rotate(d_query, cos_ref[...], -sin_ref[...]).astype(BF16)


def attend_back(blocks, query, kv, own_places, all_places, lse, grads, place, cosine, sine, heads, group):
    return call(
        functools.partial(attend_back_kernel, heads, group, len(grads), blocks),
        (shape(query.shape, BF16),)
        + (shape((sum(b.shape[0] for b in kv) // 2, kv[0].shape[1]), BF16),) * 2,
        (query, own_places, all_places, lse, cosine, sine, *grads, *kv),
        "attend_back",
        smem=(place,),
        scratch_shapes=[pltpu.VMEM(query.shape, BF16)],
    )


def gate_columns(gates, base, pair, units):
    lane = lax.broadcasted_iota(jnp.int32, gates.shape, 1)
    columns = [
        jnp.sum(jnp.where(lane == base + i, gates, 0.0), axis=1, keepdims=True) for i in range(pair)
    ]
    return jnp.concatenate(
        [jnp.broadcast_to(column, (gates.shape[0], units)) for column in columns], axis=1
    )


def whole_weight(first, own_ref, other_refs):
    pair = own_ref.shape[0]
    own = jnp.concatenate([own_ref[i] for i in range(pair)], axis=1)
    if not other_refs:
        return own
    other = jnp.concatenate([other_refs[0][i] for i in range(pair)], axis=1)
    for at, ref in enumerate(other_refs[1:], 1):
        here = jnp.concatenate([ref[i] for i in range(pair)], axis=1)
        other = jnp.where(pl.program_id(0) == at, here, other)
    return jnp.concatenate([jnp.where(first, own, other), jnp.where(first, other, own)], axis=0)


def experts_kernel(blocks, sources, counts, width, place_ref, router_ref, *refs):
    x_refs, g_refs, refs = refs[:sources], refs[sources : 2 * sources], refs[2 * sources :]
    (wg0_ref, wu0_ref, wd0_ref), refs = refs[:3], refs[3:]
    wg1_refs, refs = refs[: counts[0]], refs[counts[0] :]
    wu1_refs, refs = refs[: counts[1]], refs[counts[1] :]
    wd1_refs, refs = refs[: counts[2]], refs[counts[2] :]
    keep_ref, send_ref, own_ref, h_ref, dg_ref, du_ref, *refs = refs
    x_ref, grad_ref, gates_ref, din_acc, dgates_acc = refs
    step, steps = pl.program_id(0), pl.num_programs(0)
    pair, _, units = wg0_ref.shape
    first = place_ref[0] == 0
    base = place_ref[1] + step * pair
    rows = x_ref.shape[0] // blocks

    @pl.when(step == 0)
    def _():
        rows_in = whole_of(x_refs)
        x_ref[...] = rows_in
        grad_ref[...] = whole_of(g_refs)
        mask = grad_ref[:, width:].astype(F32)
        logits = jnp.where(mask > 0, nn(rows_in, router_ref[...]), -1e30)
        gates = mask * jnp.exp(logits - jnp.max(logits, axis=1, keepdims=True))
        gates = gates / jnp.sum(gates, axis=1, keepdims=True)
        gates_ref[...] = gates
        own_ref[...] = gates

    rows_in, rows_grad, gates = x_ref[...], grad_ref[:, :width], gates_ref[...]
    w_gate = whole_weight(first, wg0_ref, wg1_refs)
    w_up = whole_weight(first, wu0_ref, wu1_refs)
    w_down = whole_weight(first, wd0_ref, wd1_refs)
    wide = gate_columns(gates, base, pair, units)
    gate_pre, up_pre = nn(rows_in, w_gate), nn(rows_in, w_up)
    sigma = 0.5 * jnp.tanh(0.5 * gate_pre) + 0.5
    silu_gate = gate_pre * sigma
    active = silu_gate * up_pre
    h_ref[...] = (wide * active).astype(BF16)
    raw = nn(rows_grad, w_down)
    product = raw * active
    lane = lax.broadcasted_iota(jnp.int32, gates.shape, 1)
    d_gates = jnp.zeros_like(gates)
    for i in range(pair):
        column = RESID_MULT * jnp.sum(product[:, i * units : (i + 1) * units], axis=1, keepdims=True)
        d_gates = jnp.where(lane == base + i, column, d_gates)
    d_active = (RESID_MULT * wide) * raw
    d_gate_pre = (d_active * up_pre * sigma * (1.0 + gate_pre * (1.0 - sigma))).astype(BF16)
    d_up_pre = (d_active * silu_gate).astype(BF16)
    dg_ref[...], du_ref[...] = d_gate_pre, d_up_pre
    d_in = nt(d_gate_pre, w_gate) + nt(d_up_pre, w_up)

    @pl.when(step == 0)
    def _():
        din_acc[...] = d_in
        dgates_acc[...] = d_gates

    @pl.when(step > 0)
    def _():
        din_acc[...] += d_in
        dgates_acc[...] += d_gates

    @pl.when(step == steps - 1)
    def _():
        for m in range(blocks):
            ref = (keep_ref, send_ref)[m % 2]
            to, at = slice(m // 2 * rows, (m // 2 + 1) * rows), slice(m * rows, (m + 1) * rows)
            ref[to, :width] = din_acc[at].astype(BF16)
            ref[to, width:] = split_lanes(dgates_acc[at])


def held(a):
    return pl.BlockSpec(a.shape, lambda i: (0,) * len(a.shape))


def run_experts(blocks, chunks, x_blocks, g_blocks, router, place, weights, others):
    tokens, lanes = sum(b.shape[0] for b in x_blocks), g_blocks[0].shape[1]
    width = x_blocks[0].shape[1]
    count, _, units = weights[0].shape
    pair = count // chunks
    moving = lambda w: pl.BlockSpec((pair, w.shape[1], units), lambda i: (i, 0, 0))
    column = pl.BlockSpec((tokens, pair * units), lambda i: (0, i))
    outs = (
        [shape((tokens // 2, lanes), BF16)] * 2
        + [shape((tokens, LANES), F32)]
        + [shape((tokens, count * units), BF16)] * 3
    )
    flat = sum(others, [])
    return pl.pallas_call(
        functools.partial(experts_kernel, blocks, len(x_blocks), [len(o) for o in others], width),
        grid=(chunks,),
        out_shape=tuple(outs),
        in_specs=[pl.BlockSpec(memory_space=pltpu.SMEM), held(router)]
        + [held(b) for b in x_blocks + g_blocks]
        + [moving(w) for w in weights]
        + [held(o) for o in flat],
        out_specs=tuple(held(o) for o in outs[:3]) + (column,) * 3,
        scratch_shapes=[
            pltpu.VMEM((tokens, width), BF16),
            pltpu.VMEM((tokens, lanes), BF16),
            pltpu.VMEM((tokens, LANES), F32),
            pltpu.VMEM((tokens, width), F32),
            pltpu.VMEM((tokens, LANES), F32),
        ],
        compiler_params=pltpu.CompilerParams(vmem_limit_bytes=VMEM_BYTES),
        cost_estimate=cost("experts"),
        name="experts",
    )(place, router, *x_blocks, *g_blocks, *weights, *flat)


def grads_kernel(sources, parts, width, place_ref, *refs):
    x_refs, g_refs, refs = refs[:sources], refs[sources : 2 * sources], refs[2 * sources :]
    h_refs, dg_refs, du_refs = (refs[i * parts : (i + 1) * parts] for i in range(3))
    grad_refs = refs[3 * parts :]
    pair, half, units = grad_refs[0].shape
    first = place_ref[0] == 0

    def halves(grad, own_ref, other_ref):
        own = jnp.where(first, grad[:half], grad[half:]).astype(BF16)
        other = jnp.where(first, grad[half:], grad[:half]).astype(BF16)
        for i in range(pair):
            own_ref[i] = own[:, i * units : (i + 1) * units]
            other_ref[i] = other[:, i * units : (i + 1) * units]

    rows_in, rows_grad = whole_of(x_refs), whole_of(g_refs)[:, :width]
    halves(RESID_MULT * tn(rows_grad, whole_of(h_refs)), grad_refs[4], grad_refs[5])
    halves(tn(rows_in, whole_of(dg_refs)), grad_refs[0], grad_refs[1])
    halves(tn(rows_in, whole_of(du_refs)), grad_refs[2], grad_refs[3])


def run_grads(x_blocks, g_blocks, place, hidden, d_gate, d_up, dims, chunks):
    parts, tokens = len(hidden), sum(b.shape[0] for b in x_blocks)
    count, half, units = dims
    pair = count // chunks
    width = x_blocks[0].shape[1]
    moving = pl.BlockSpec((pair, half, units), lambda i: (i, 0, 0))
    column = pl.BlockSpec((tokens // parts, pair * units), lambda i: (0, i))
    return pl.pallas_call(
        functools.partial(grads_kernel, len(x_blocks), parts, width),
        grid=(chunks,),
        out_shape=(shape(dims, BF16),) * 6,
        in_specs=[pl.BlockSpec(memory_space=pltpu.SMEM)]
        + [held(b) for b in x_blocks + g_blocks]
        + [column] * (3 * parts),
        out_specs=(moving,) * 6,
        compiler_params=pltpu.CompilerParams(vmem_limit_bytes=VMEM_BYTES),
        cost_estimate=cost("grads"),
        name="grads",
    )(place, *x_blocks, *g_blocks, *hidden, *d_gate, *d_up)


def outputs_kernel(blocks, parts, chunks, place_ref, wd0_ref, *refs):
    h_refs, refs = refs[:parts], refs[parts:]
    wd1_refs, out_refs, out_acc = refs[:chunks], refs[chunks:-1], refs[-1]
    step, steps = pl.program_id(0), pl.num_programs(0)
    out = nt(whole_of(h_refs), whole_weight(place_ref[0] == 0, wd0_ref, wd1_refs))

    @pl.when(step == 0)
    def _():
        out_acc[...] = out

    @pl.when(step > 0)
    def _():
        out_acc[...] += out

    @pl.when(step == steps - 1)
    def _():
        rows = out_acc.shape[0] // blocks
        for m in range(blocks):
            out_refs[m % 2 * parts + m // 2][...] = out_acc[m * rows : (m + 1) * rows].astype(BF16)


def run_outputs(place, hidden, w_own, others):
    parts, chunks = len(hidden), len(others)
    count, half, units = w_own.shape
    pair, tokens, width = count // chunks, parts * hidden[0].shape[0], 2 * half
    outs = (shape((tokens // parts // 2, width), BF16),) * (2 * parts)
    column = pl.BlockSpec((tokens // parts, pair * units), lambda i: (0, i))
    return pl.pallas_call(
        functools.partial(outputs_kernel, 2 * parts, parts, chunks),
        grid=(chunks,),
        out_shape=outs,
        in_specs=[
            pl.BlockSpec(memory_space=pltpu.SMEM),
            pl.BlockSpec((pair, half, units), lambda i: (i, 0, 0)),
        ]
        + [column] * parts
        + [held(o) for o in others],
        out_specs=tuple(held(o) for o in outs),
        scratch_shapes=[pltpu.VMEM((tokens, width), F32)],
        compiler_params=pltpu.CompilerParams(vmem_limit_bytes=VMEM_BYTES),
        cost_estimate=cost("outputs"),
        name="outputs",
    )(place, w_own, *hidden, *others)


def rms_back(rows, gain, grad):
    scale = lax.rsqrt(jnp.mean(rows * rows, axis=-1, keepdims=True) + NORM_EPS)
    d_gain = jnp.sum(grad * rows * scale, axis=0, keepdims=True)
    pulled = grad * gain
    mean = jnp.mean(pulled * rows, axis=-1, keepdims=True)
    return scale * pulled - rows * (scale * scale * scale) * mean, d_gain


def body(
    hidden_in,
    positions,
    routes,
    out_grad,
    attn_gain,
    query_weight,
    key_matrix,
    value_matrix,
    out_weight,
    moe_gain,
    router_weight,
    gate_weight,
    up_weight,
    down_weight,
):
    shards, contexts, tensors = (lax.axis_size(a) for a in ("shards", "context", "tensor"))
    shard, context, tensor = (lax.axis_index(a) for a in ("shards", "context", "tensor"))
    owners = shards * contexts
    steps = stepped()
    owner = shard * contexts + context if steps else 0 * shard
    flip = context if steps else 0 * context
    rows, width = hidden_in.shape[1:]
    chunk, quarter = width // owners, rows // tensors
    wide, narrow = query_weight.shape[1], key_matrix.shape[1]
    heads, group = wide // HEAD_SIZE, wide // narrow
    expert_count, local_experts = router_weight.shape[1], gate_weight.shape[0]
    columns = 2 * wide + 2 * narrow
    gates_at = tensor if steps else context * tensors + tensor
    place = jnp.stack([shard, context * local_experts, flip, owner, tensor, gates_at])
    place = place.astype(jnp.int32)

    packed = jnp.concatenate(
        [
            jnp.concatenate([query_weight, key_matrix, value_matrix, out_weight], axis=1),
            jnp.pad(
                jnp.concatenate([attn_gain, moe_gain])[None], ((0, 7), (0, columns - 2 * chunk))
            ),
            jnp.pad(
                router_weight.reshape(8, chunk * expert_count // 8),
                ((0, 0), (0, columns - chunk * expert_count // 8)),
            ),
        ],
        axis=0,
    )
    grad_rows = out_grad[0]
    names = jnp.arange(LANES, dtype=jnp.int32)
    mask = jnp.any(routes[0][:, :, None] == names[None, None, :], axis=1).astype(BF16)
    gathered = gather_owners(packed)
    if steps:
        even, odd = gathered[:4], gathered[4:]
        pieces = [p for pair in zip(even, odd) for p in pair]
        gain_a = jnp.concatenate([p[chunk : chunk + 1, :chunk] for p in pieces], axis=1).astype(F32)
    else:
        stack = gathered[0]
        pieces = [stack[:, :chunk].reshape(width, columns)]
        gain_a = stack[:, chunk, :chunk].reshape(1, width).astype(F32)

    chunks = 2 if local_experts % 2 == 0 else 1
    size = local_experts // chunks
    weights = [lax.all_gather(w, "shards", axis=1, tiled=True) for w in (gate_weight, up_weight)]
    weights.append(down_weight)
    down_other = [swap(down_weight[i * size : (i + 1) * size], "shards", 1) for i in range(chunks)]
    others = [[], [], down_other]

    place_all = positions[0].reshape(contexts, rows)
    own_places = cut(place_all, context, 1).reshape(rows, 1)
    if steps:
        place_all = jnp.concatenate(xor_blocks([place_all[i] for i in range(contexts)], context))
    all_places = place_all.reshape(1, contexts * rows)
    half = HEAD_SIZE // 2
    frequency = ROPE_BASE ** (-2.0 * jnp.arange(half, dtype=F32) / HEAD_SIZE)
    angles = own_places.astype(F32) * frequency[None, :]
    cosine, sine = jnp.cos(angles), jnp.sin(angles)
    cosine = jnp.concatenate([cosine] * 4, axis=1)
    sine = jnp.concatenate([-sine, sine] * 2, axis=1)

    hidden = hidden_in[0]
    hidden_rel = hidden
    if steps:
        hidden_rel = jnp.concatenate(xor_blocks(columns_of(hidden, owners), owner), axis=1)
    normed_a, query, kv, w_qkv = project(
        hidden_rel, gain_a, pieces, cosine, sine, wide, narrow, chunk if steps else width
    )
    kv_all = gather_context(kv)
    attended, lse = attend(query, kv_all, own_places, all_places, heads, group)

    if steps:
        evens = jnp.concatenate([p[:chunk, columns - wide :] for p in even], axis=0)
        bit = 1
        while bit < tensors:
            evens = jnp.concatenate([evens, after(swap(evens, "tensor", bit), query)], axis=0)
            bit *= 2
        w_out = call(
            functools.partial(assemble_kernel, (0, 2, 4, 6, 1, 3, 5, 7), chunk),
            [shape((width, wide * tensors), BF16)],
            (evens, swap(after(evens, attended), "context", 1)),
            "assemble",
            smem=(place,),
        )[0]
        late = [after(p, query) for p in pieces]
        gain_m = [p[chunk : chunk + 1, chunk : 2 * chunk] for p in late]
        gain_m = jnp.concatenate(xor_blocks(gain_m, owner), axis=1).astype(F32)
        router = [p[chunk + 8 : chunk + 16, : chunk * expert_count // 8] for p in late]
        router = jnp.concatenate(xor_blocks(router, owner), axis=0).reshape(width, expert_count)
    else:
        own = pieces[0][:, columns - wide :]
        w_out = jnp.concatenate([own] + [turn(own, k) for k in range(1, tensors)], axis=1)
        gain_m = stack[:, chunk, chunk : 2 * chunk].reshape(1, width).astype(F32)
        router = stack[:, chunk + 8 :, : chunk * expert_count // 8].reshape(width, expert_count)
    router = jnp.pad(router, ((0, 0), (0, LANES - expert_count)))
    attended_all = [attended] + [turn(attended, k) for k in range(1, tensors)]
    middle, normed_m = call(
        middle_kernel,
        (shape(hidden.shape, F32), shape(hidden.shape, BF16)),
        (after(hidden, router, down_other[0]), gain_m, w_out, *attended_all),
        "middle",
    )

    if steps:
        across = swap(normed_m, "context", 2)
        x_blocks = [normed_m, swap(normed_m, "context", 1)]
    else:
        x_blocks = gather_context(normed_m)
    g_blocks = gather_context(jnp.concatenate([grad_rows, mask], axis=1))
    run = lambda xs, gs: run_experts(2, chunks, xs, gs, router, place, weights, others)
    if steps:
        found = [run(x_blocks, g_blocks[:2])]
        across = after(across, found[0][0])
        x_blocks += [across, swap(across, "context", 1)]
        found.append(run(x_blocks[2:], g_blocks[2:]))
    else:
        parts = [
            ([cut(x_blocks[0], i, PART_ROWS)], [cut(g_blocks[0], i, PART_ROWS)])
            for i in range(contexts * rows // PART_ROWS)
        ]
        found = [run(xs, gs) for xs, gs in parts]
    gates = found[0][2] if steps else jnp.concatenate([f[2] for f in found], axis=0)

    def to_quarters(kept, sent, form):
        if steps:
            core = [swap(b, "context", 1) for b in sent]
            send = fold((kept[1], core[1]), place, width, 0)[0]
            return send, fold((kept[0], core[0], swap(send, "context", 2)), place, width, form)
        whole = jnp.concatenate([b for pair in zip(kept, sent) for b in pair], axis=0)
        own = lax.psum_scatter(whole, "context", scatter_dimension=0, tiled=True)
        return own, fold((own,), place, width, form)

    early, d_normed = to_quarters([f[0] for f in found], [f[1] for f in found], tensors)
    hidden_parts = [[f[3] for f in found]] if steps else [[f[3]] for f in found]
    hidden_parts = [[after(h[0], d_normed[0])] + h[1:] for h in hidden_parts]
    outputs = [run_outputs(place, h, down_weight, down_other) for h in hidden_parts]
    if steps:
        outputs = [(outputs[0][i], outputs[0][2 + i]) for i in range(2)]
    dims = gate_weight.shape
    if steps:
        columns_in = [[f[i] for f in found] for i in (3, 4, 5)]
        columns_in[0][0] = after(columns_in[0][0], early)
        grads = run_grads(x_blocks, g_blocks, place, *columns_in, dims, chunks)
    else:
        grads = [
            run_grads(xs, gs, place, [f[3]], [f[4]], [f[5]], dims, chunks)
            for f, (xs, gs) in zip(found, parts)
        ]
        grads = [sum(g.astype(F32) for g in one).astype(BF16) for one in zip(*grads)]

    parts = [d_normed[0]] + [turn(d_normed[k], k) for k in range(1, tensors)]
    outs = (
        shape((quarter, width), F32),
        shape((quarter, width), BF16),
        shape((1, width), F32),
        shape((width, LANES), F32),
        shape((quarter, wide), BF16),
    ) + (shape((quarter, wide + width), BF16),) * (tensors - 1)
    own = lambda lanes: pl.BlockSpec((quarter, lanes), lambda i, at: (at[4], 0))
    gates_own = pl.BlockSpec((quarter, LANES), lambda i, at: (at[5], 0))
    full = lambda a: pl.BlockSpec(a.shape, lambda i, at: (0, 0))
    d_middle, d_attn, d_gain_m, d_router, *d_attended = pl.pallas_call(
        functools.partial(middle_back_kernel, width),
        out_shape=outs,
        grid_spec=pltpu.PrefetchScalarGridSpec(
            num_scalar_prefetch=1,
            grid=(1,),
            in_specs=[own(width), own(width), full(gain_m), own(width), gates_own, full(router), full(w_out)]
            + [full(p) for p in parts],
            out_specs=tuple(full(o) for o in outs),
        ),
        compiler_params=pltpu.CompilerParams(vmem_limit_bytes=VMEM_BYTES),
        cost_estimate=cost("middle_back"),
        name="middle_back",
    )(place, middle, normed_m, gain_m, grad_rows, after(gates, outputs[0][0], grads[0]), router, w_out, *parts)

    came = [swap(grads[i], "shards", 1) for i in (5, 1, 3)]

    d_attended = [turn(d, k) if k else d for k, d in enumerate(d_attended)]
    out_early, moe_out = to_quarters(
        *([after(o[i], d_middle) for o in outputs] for i in range(2)), 0
    )
    d_query, d_kv, d_kv_send = attend_back(
        contexts if steps else 2,
        after(query, came[0], out_early),
        kv_all,
        own_places,
        all_places,
        lse,
        d_attended,
        place,
        cosine,
        sine,
        heads,
        group,
    )
    exchange = lambda x: lax.all_to_all(x, "tensor", 0, 0, tiled=True)
    moe_rows = exchange(moe_out[0].reshape(tensors, quarter, width))
    moe_rows = jnp.sum(moe_rows.astype(F32), axis=0)
    block_out = (cut(middle, tensor, quarter) + RESID_MULT * moe_rows).astype(BF16)
    if steps:
        d_kv = d_kv.astype(F32) + swap(d_kv_send, "context", 1).astype(F32)
        d_kv, d_kv_send = d_kv[:rows], swap(d_kv[rows:].astype(BF16), "context", 2)
    else:
        d_kv = jnp.concatenate([d_kv, d_kv_send], axis=0)
        d_kv = lax.psum_scatter(d_kv, "context", scatter_dimension=0, tiled=True)
        d_kv_send = jnp.zeros_like(d_kv)
    *d_normed, d_lin, d_gain_a = call(
        functools.partial(project_back_kernel, narrow),
        [shape((quarter, width), F32)]
        + [shape((quarter, width), BF16)] * (tensors - 1)
        + [shape((rows, wide + 2 * narrow), BF16), shape((1, width), F32)],
        (after(d_query, came[1], moe_out[0]), d_kv, d_kv_send, cosine[:, :narrow], sine[:, :narrow], w_qkv, hidden_rel),
        "project_back",
        smem=(place,),
        scratch_shapes=[pltpu.VMEM((rows, width), F32)],
    )
    parts = [turn(d_normed[k], k) for k in range(1, tensors)]
    if steps:
        kept, sent = call(
            functools.partial(weights_back_kernel, OWNER_ORDER, chunk),
            [shape((width // 2, columns), BF16)] * 2,
            (normed_a, after(d_lin, moe_rows), attended, d_attn, *d_attended[1:]),
            "weights_back",
            smem=(place,),
            scratch_shapes=[pltpu.VMEM((rows, width), BF16), pltpu.VMEM((width, wide), F32)],
        )
        tie, d_weights = scatter_owners(kept, sent, BF16)
    d_normed = d_normed[0] + sum(p.astype(F32) for p in parts)
    d_rows, _unused = rms_back(
        cut(hidden_rel, tensor, quarter).astype(F32), gain_a, d_normed
    )
    if steps:
        d_rows = jnp.concatenate(xor_blocks(columns_of(d_rows, owners), owner), axis=1)
    in_grad = gather_tensor((d_middle + d_rows).astype(BF16)).astype(F32)

    block_out = exchange(jnp.broadcast_to(after(block_out, d_rows)[None], (tensors, quarter, width)))
    block_out = block_out.reshape(rows, width)

    expert_grads = [
        after(own, d_rows).astype(F32) + other.astype(F32)
        for own, other in ((grads[0], came[1]), (grads[2], came[2]), (grads[4], came[0]))
    ]
    small = jnp.concatenate([d_gain_m, d_router[:, :expert_count].T], axis=0)
    d_gain_a = after(d_gain_a, d_normed)
    if steps:
        small = xor_blocks(columns_of(small, owners), owner)
        small = [
            jnp.concatenate([a, b], axis=0) for a, b in zip(columns_of(d_gain_a, owners), small)
        ]
        small = [jnp.pad(b, ((0, -b.shape[0] % 8), (0, 0))) for b in small]
        kept, sent = (
            jnp.concatenate([small[r] for r in OWNER_ORDER[i : i + 4]], axis=0) for i in (0, 4)
        )
        small = scatter_owners(kept, sent, F32)[1]
    else:
        over = ("shards", "context")
        attn_rows = [d_attn] + [d[:, wide:] for d in d_attended[1:]]
        attn_rows = jnp.concatenate(xor_blocks(attn_rows, tensor), axis=0)
        d_weights = jnp.concatenate([tn(normed_a, d_lin), tn(attn_rows, attended)], axis=1)
        d_weights = lax.psum_scatter(
            d_weights.astype(BF16), over, scatter_dimension=0, tiled=True
        ).astype(F32)
        small = jnp.concatenate([d_gain_a, small], axis=0)
        small = jnp.swapaxes(small.reshape(-1, owners, chunk), 0, 1)
        small = lax.psum_scatter(small, over, scatter_dimension=0)
    small = butterfly(small)
    return (
        block_out[None],
        in_grad[None],
        small[0],
        d_weights[:, :wide],
        d_weights[:, wide : wide + narrow],
        d_weights[:, wide + narrow : wide + 2 * narrow],
        d_weights[:, wide + 2 * narrow :],
        small[1],
        small[2 : 2 + expert_count].T,
        expert_grads[0],
        expert_grads[1],
        expert_grads[2],
    )


def solution(mesh):
    owned = ("shards", "context")
    rows = P("shards", "context", None)
    split = P(owned, "tensor")
    expert = P("context", "shards", "tensor")
    return jax.shard_map(
        body,
        mesh=mesh,
        in_specs=(
            rows,
            P("shards", None),
            rows,
            rows,
            P(owned),
            split,
            split,
            split,
            split,
            P(owned),
            P(owned, None),
            expert,
            expert,
            expert,
        ),
        out_specs=(
            rows,
            rows,
            P(owned),
            split,
            split,
            split,
            split,
            P(owned),
            P(owned, None),
            expert,
            expert,
            expert,
        ),
        check_vma=False,
    )
```

```python
import functools

import jax
import jax.numpy as jnp
from jax import lax
from jax.experimental import pallas as pl
from jax.experimental.pallas import tpu as pltpu
from jax.sharding import PartitionSpec as P

HEAD_SIZE = 64
NORM_EPS = 1e-06
ATTN_MULT = 0.015625
RESID_MULT = 0.22
ROPE_BASE = 10000.0
F32 = jnp.float32
BF16 = jnp.bfloat16
VMEM_BYTES = 56 * 1024 * 1024
PART_ROWS = 1024
MICROSECONDS = {
    "project": 3,
    "assemble": 3,
    "middle": 4,
    "fold": 2.5,
    "middle_back": 4.5,
    "project_back": 3,
    "weights_back": 3,
    "attend": 4,
    "attend_back": 6,
    "experts": 12,
    "grads": 12,
    "outputs": 9,
}
LANES = 128


def swap(x, axis, bit):
    devices = lax.axis_size(axis)
    return lax.ppermute(x, axis, [(i, i ^ bit) for i in range(devices)])


def turn(x, k):
    return swap(x, "tensor", k)


def stepped():
    return lax.axis_size("context") == 4 and lax.axis_size("shards") == 2


def after(x, *others):
    return lax.optimization_barrier((x,) + others)[0]


def gather_context(x):
    if not stepped():
        return [lax.all_gather(x, "context", axis=0, tiled=True)]
    across = swap(x, "context", 2)
    return [x, swap(x, "context", 1), across, swap(across, "context", 1)]


def swap_tensor(x, bit):
    return swap(x, "tensor", bit)


def gather_owners(x):
    if not stepped():
        return [lax.all_gather(x, ("shards", "context"))]
    far = []
    for m in (2, 4, 6):
        far.append(lax.ppermute(x, ("shards", "context"), [(i, i ^ m) for i in range(8)]))
    near = swap(x, "context", 1)
    odd = swap(jnp.concatenate(far, axis=0), "context", 1)
    size = x.shape[0]
    return [x] + far + [near] + [odd[i * size : (i + 1) * size] for i in range(3)]


OWNER_ORDER = (0, 4, 2, 6, 1, 5, 3, 7)


def scatter_owners(keep, send, travel):
    size = keep.shape[0] // 4
    total = keep.astype(F32) + swap(send.astype(travel), "context", 1).astype(F32)
    far = swap(total[2 * size :].astype(travel), "context", 2).astype(F32)
    total = total[: 2 * size] + far
    return total, total[:size] + swap(total[size:].astype(travel), "shards", 1).astype(F32)


def butterfly(x):
    bit = 1
    while bit < lax.axis_size("tensor"):
        x = x + lax.ppermute(x, "tensor", [(i, i ^ bit) for i in range(lax.axis_size("tensor"))])
        bit *= 2
    return x


def xor_blocks(pieces, index):
    pieces, bit = list(pieces), 1
    while bit < len(pieces):
        flag = (index & bit) != 0
        pieces = [jnp.where(flag, pieces[i ^ bit], pieces[i]) for i in range(len(pieces))]
        bit *= 2
    return pieces


def columns_of(x, count):
    size = x.shape[1] // count
    return [x[:, i * size : (i + 1) * size] for i in range(count)]


def cut(x, index, size):
    return lax.dynamic_slice_in_dim(x, index * size, size, axis=0)


def gather_tensor(x):
    devices, me = lax.axis_size("tensor"), lax.axis_index("tensor")
    size = x.shape[0]
    whole = jnp.zeros((size * devices,) + x.shape[1:], x.dtype)
    for k in range(devices):
        piece = turn(x, k) if k else x
        whole = lax.dynamic_update_slice_in_dim(whole, piece, (me ^ k) * size, axis=0)
    return whole


def nn(a, b):
    return lax.dot_general(a, b, (((1,), (0,)), ((), ())), preferred_element_type=F32)


def tn(a, b):
    return lax.dot_general(a, b, (((0,), (0,)), ((), ())), preferred_element_type=F32)


def nt(a, b):
    return lax.dot_general(a, b, (((1,), (1,)), ((), ())), preferred_element_type=F32)


def vmem():
    return pl.BlockSpec(memory_space=pltpu.VMEM)


def rotate(x, cosine, sine):
    lanes = x.shape[1]
    times = lanes // cosine.shape[1]
    lane = lax.broadcasted_iota(jnp.int32, x.shape, 1)
    half = HEAD_SIZE // 2
    partner = jnp.where(
        lane % HEAD_SIZE < half, pltpu.roll(x, lanes - half, 1), pltpu.roll(x, half, 1)
    )
    return x * jnp.concatenate([cosine] * times, 1) + partner * jnp.concatenate([sine] * times, 1)


def cost(name):
    flops = int(MICROSECONDS[name] * 1.15e9)
    return pl.CostEstimate(flops=flops, transcendentals=0, bytes_accessed=0)


def call(kernel, out_shape, operands, name, smem=(), **more):
    specs = [pl.BlockSpec(memory_space=pltpu.SMEM)] * len(smem) + [vmem()] * len(operands)
    return pl.pallas_call(
        kernel,
        out_shape=tuple(out_shape),
        in_specs=specs,
        out_specs=(vmem(),) * len(out_shape),
        compiler_params=pltpu.CompilerParams(vmem_limit_bytes=VMEM_BYTES),
        cost_estimate=cost(name),
        name=name,
        **more,
    )(*smem, *operands)


def shape(dims, dtype):
    return jax.ShapeDtypeStruct(tuple(dims), dtype)


def project_kernel(wide, narrow, chunk, hid_ref, gain_ref, cos_ref, sin_ref, *refs):
    *pieces, norm_ref, q_ref, kv_ref, w_ref = refs
    for i, piece in enumerate(pieces):
        w_ref[i * chunk : (i + 1) * chunk] = piece[:chunk, : w_ref.shape[1]]
    hid = hid_ref[...].astype(F32)
    scale = lax.rsqrt(jnp.mean(hid * hid, axis=1, keepdims=True) + NORM_EPS)
    normed = (hid * scale * gain_ref[...]).astype(BF16)
    norm_ref[...] = normed
    lin = nn(normed, w_ref[...])
    turned = rotate(lin[:, : wide + narrow], cos_ref[...], sin_ref[...]).astype(BF16)
    q_ref[...] = turned[:, :wide] * ATTN_MULT
    kv_ref[:, :narrow] = turned[:, wide:]
    kv_ref[:, narrow:] = lin[:, wide + narrow :].astype(BF16)


def project(hidden, gain, pieces, cosine, sine, wide, narrow, chunk):
    rows, width = hidden.shape
    return call(
        functools.partial(project_kernel, wide, narrow, chunk),
        (
            shape((rows, width), BF16),
            shape((rows, wide), BF16),
            shape((rows, 2 * narrow), BF16),
            shape((width, wide + 2 * narrow), BF16),
        ),
        (hidden, gain, cosine, sine, *pieces),
        "project",
    )


def assemble_kernel(order, chunk, place_ref, even_ref, odd_ref, out_ref):
    wide = even_ref.shape[1]
    size = len(order) // 2 * chunk
    for k in range(even_ref.shape[0] // size):
        for at, r in enumerate(order):
            start = k * size + at % (len(order) // 2) * chunk
            rows = pl.ds(pl.multiple_of((place_ref[3] ^ r) * chunk, chunk), chunk)
            source = (even_ref, odd_ref)[r % 2]
            out_ref[rows, k * wide : (k + 1) * wide] = source[start : start + chunk]


def middle_kernel(hid_ref, gain_ref, w_ref, *refs):
    *att_refs, mid_ref, norm_ref = refs
    attended = jnp.concatenate([r[...] for r in att_refs], axis=1)
    middle = hid_ref[...].astype(F32) + RESID_MULT * nt(attended, w_ref[...])
    scale = lax.rsqrt(jnp.mean(middle * middle, axis=1, keepdims=True) + NORM_EPS)
    mid_ref[...] = middle
    norm_ref[...] = (middle * scale * gain_ref[...]).astype(BF16)


def split_lanes(x):
    high = x.astype(BF16)
    low = (x - high.astype(F32)).astype(BF16).astype(F32)
    return (high.astype(F32) + pltpu.roll(low, LANES // 2, 1)).astype(BF16)


def join_lanes(x):
    lane = lax.broadcasted_iota(jnp.int32, x.shape, 1)
    return jnp.where(lane < LANES // 2, x + pltpu.roll(x, LANES // 2, 1), 0.0)


def fold_kernel(width, quarters, terms, place_ref, *refs):
    total = refs[0][...].astype(F32)
    for ref in refs[1:terms]:
        total = total + ref[...].astype(F32)
    if not quarters:
        ref = refs[terms]
        ref[:, :width] = total[:, :width].astype(BF16)
        if total.shape[1] > width:
            ref[:, width:] = split_lanes(join_lanes(total[:, width:]))
        return
    own_ref, *send_refs, total_ref = refs[terms:]
    if total.shape[1] > width:
        total = jnp.concatenate([total[:, :width], join_lanes(total[:, width:])], axis=1)
    total_ref[...] = total
    size = own_ref.shape[0]

    def part(index):
        index = place_ref[4] ^ index
        return total_ref[pl.ds(pl.multiple_of(index * size, size), size)]

    own_ref[...] = part(0)
    for k, ref in enumerate(send_refs, 1):
        found = part(k)
        ref[:, :width] = found[:, :width].astype(BF16)
        if found.shape[1] > width:
            ref[:, width:] = split_lanes(found[:, width:])


def fold(terms, place, width, quarters):
    rows, lanes = terms[0].shape
    size = rows // max(quarters, 1)
    outs = [shape((size, lanes), BF16)]
    if quarters:
        outs = [shape((size, lanes), F32)] + outs * (quarters - 1)
    return call(
        functools.partial(fold_kernel, width, quarters, len(terms)),
        outs,
        terms,
        "fold",
        smem=(place,),
        scratch_shapes=[pltpu.VMEM((rows, lanes), F32)] if quarters else [],
    )


def middle_back_kernel(width, _place_ref, mid_ref, norm_ref, gain_ref, grad_ref, gates_ref, router_ref, w_ref, *refs):
    outs = (len(refs) - 4) // 2
    parts, refs = refs[:outs], refs[outs:]
    dmid_ref, dattn_ref, dgain_ref, drouter_ref = refs[:4]
    total = parts[0][...]
    for part in parts[1:]:
        total = total + part[...].astype(F32)
    gates, d_gates = gates_ref[...], join_lanes(total[:, width:])
    d_picked = gates * (d_gates - jnp.sum(gates * d_gates, axis=1, keepdims=True))
    d_logits = d_picked.astype(BF16)
    drouter_ref[...] = tn(norm_ref[...], d_logits)
    d_normed = total[:, :width] + nt(d_logits, router_ref[...])
    d_rows, d_gain = rms_back(mid_ref[...], gain_ref[...], d_normed)
    d_middle = grad_ref[...].astype(F32) + d_rows
    d_attn = (RESID_MULT * d_middle).astype(BF16)
    dmid_ref[...], dattn_ref[...], dgain_ref[...] = d_middle, d_attn, d_gain
    d_attended = nn(d_attn, w_ref[...]).astype(BF16)
    wide = d_attended.shape[1] // outs
    for k, ref in enumerate(refs[4:]):
        ref[:, :wide] = d_attended[:, k * wide : (k + 1) * wide]
        if k:
            ref[:, wide:] = d_attn


def project_back_kernel(narrow, place_ref, dq_ref, keep_ref, came_ref, cos_ref, sin_ref, w_ref, hid_ref, *refs):
    own_ref, *send_refs, dlin_ref, dgain_ref, total_ref = refs
    d_kv = keep_ref[...].astype(F32) + came_ref[...].astype(F32)
    d_key = rotate(d_kv[:, :narrow], cos_ref[...], -sin_ref[...])
    d_lin = jnp.concatenate(
        [dq_ref[...], d_key.astype(BF16), d_kv[:, narrow:].astype(BF16)], axis=1
    )
    dlin_ref[...] = d_lin
    d_normed = nt(d_lin, w_ref[...])
    total_ref[...] = d_normed
    hid = hid_ref[...].astype(F32)
    scale = lax.rsqrt(jnp.mean(hid * hid, axis=1, keepdims=True) + NORM_EPS)
    dgain_ref[...] = jnp.sum(d_normed * hid * scale, axis=0, keepdims=True)
    size, quarters = own_ref.shape[0], 1 + len(send_refs)

    def part(k):
        index = place_ref[4] ^ k
        return total_ref[pl.ds(pl.multiple_of(index * size, size), size)]

    own_ref[...] = part(0)
    for k, ref in enumerate(send_refs, 1):
        ref[...] = part(k).astype(BF16)


def weights_back_kernel(order, chunk, place_ref, norm_ref, dlin_ref, att_ref, *refs):
    lin = tn(norm_ref[...], dlin_ref[...]).astype(BF16)
    *dattn_refs, keep_ref, send_ref, rows_ref, scratch_ref = refs
    size = dattn_refs[0].shape[0]
    for k, ref in enumerate(dattn_refs):
        columns = slice(ref.shape[1] - rows_ref.shape[1], None)
        rows_ref[pl.ds(pl.multiple_of((place_ref[4] ^ k) * size, size), size)] = ref[:, columns]
    scratch_ref[...] = tn(rows_ref[...], att_ref[...])
    split = lin.shape[1]
    for at, r in enumerate(order):
        ref = (keep_ref, send_ref)[r % 2]
        start = at % (len(order) // 2) * chunk
        rows = pl.ds(pl.multiple_of((place_ref[3] ^ r) * chunk, chunk), chunk)
        ref[start : start + chunk, :split] = lin[r * chunk : (r + 1) * chunk]
        ref[start : start + chunk, split:] = scratch_ref[rows].astype(BF16)


def whole_of(refs):
    return jnp.concatenate([r[...] for r in refs], axis=0) if len(refs) > 1 else refs[0][...]


def attend_kernel(heads, group, q_ref, own_ref, all_ref, *refs):
    *kv_refs, out_ref, lse_ref = refs
    kv = whole_of(kv_refs)
    narrow = kv.shape[1] // 2
    bias = jnp.where(all_ref[...] <= own_ref[...], 0.0, -1e30)
    for h in range(heads):
        at, kv_at = h * HEAD_SIZE, (h // group) * HEAD_SIZE
        key = kv[:, kv_at : kv_at + HEAD_SIZE]
        value = kv[:, narrow + kv_at : narrow + kv_at + HEAD_SIZE]
        scores = nt(q_ref[:, at : at + HEAD_SIZE], key) + bias
        top = jnp.max(scores, axis=1, keepdims=True)
        weights = jnp.exp(scores - top)
        total = jnp.sum(weights, axis=1, keepdims=True)
        out = nn(weights.astype(BF16), value) / total
        out_ref[:, at : at + HEAD_SIZE] = out.astype(BF16)
        lse_ref[:, h : h + 1] = top + jnp.log(total)


def attend(query, kv, own_places, all_places, heads, group):
    return call(
        functools.partial(attend_kernel, heads, group),
        (shape(query.shape, BF16), shape((query.shape[0], heads), F32)),
        (query, own_places, all_places, *kv),
        "attend",
    )


def attend_back_kernel(
    heads, group, quarters, blocks, place_ref, q_ref, own_ref, all_ref, lse_ref, cos_ref, sin_ref, *refs
):
    grads, refs = refs[:quarters], refs[quarters:]
    *kv_refs, dq_ref, keep_ref, send_ref, grad_ref = refs
    size = grads[0].shape[0]
    for k, ref in enumerate(grads):
        index = place_ref[4] ^ k
        grad_ref[pl.ds(pl.multiple_of(index * size, size), size)] = ref[:, : grad_ref.shape[1]]
    kv = whole_of(kv_refs)
    narrow = kv.shape[1] // 2
    bias = jnp.where(all_ref[...] <= own_ref[...], 0.0, -1e30)
    d_queries, d_keys, d_values = [], [], []
    for pair in range(heads // group):
        kv_at = pair * HEAD_SIZE
        key = kv[:, kv_at : kv_at + HEAD_SIZE]
        value = kv[:, narrow + kv_at : narrow + kv_at + HEAD_SIZE]
        d_key, d_value = 0.0, 0.0
        for h in range(pair * group, (pair + 1) * group):
            at = h * HEAD_SIZE
            query, grad = q_ref[:, at : at + HEAD_SIZE], grad_ref[:, at : at + HEAD_SIZE]
            probs = jnp.exp(nt(query, key) + bias - lse_ref[:, h : h + 1])
            d_probs = nt(grad, value)
            delta = jnp.sum(probs * d_probs, axis=1, keepdims=True)
            d_scores = (probs * (d_probs - delta)).astype(BF16)
            d_queries.append(nn(d_scores, key) * ATTN_MULT)
            d_key = d_key + tn(d_scores, query)
            d_value = d_value + tn(probs.astype(BF16), grad)
        d_keys.append(d_key)
        d_values.append(d_value)
    d_kv = jnp.concatenate(d_keys + d_values, axis=1).astype(BF16)
    rows = d_kv.shape[0] // blocks
    for m in range(blocks):
        ref = (keep_ref, send_ref)[m % 2]
        ref[m // 2 * rows : (m // 2 + 1) * rows] = d_kv[m * rows : (m + 1) * rows]
    d_query = jnp.concatenate(d_queries, axis=1)
    dq_ref[...] = rotate(d_query, cos_ref[...], -sin_ref[...]).astype(BF16)


def attend_back(blocks, query, kv, own_places, all_places, lse, grads, place, cosine, sine, heads, group):
    return call(
        functools.partial(attend_back_kernel, heads, group, len(grads), blocks),
        (shape(query.shape, BF16),)
        + (shape((sum(b.shape[0] for b in kv) // 2, kv[0].shape[1]), BF16),) * 2,
        (query, own_places, all_places, lse, cosine, sine, *grads, *kv),
        "attend_back",
        smem=(place,),
        scratch_shapes=[pltpu.VMEM(query.shape, BF16)],
    )


def gate_columns(gates, base, pair, units):
    lane = lax.broadcasted_iota(jnp.int32, gates.shape, 1)
    columns = [
        jnp.sum(jnp.where(lane == base + i, gates, 0.0), axis=1, keepdims=True) for i in range(pair)
    ]
    return jnp.concatenate(
        [jnp.broadcast_to(column, (gates.shape[0], units)) for column in columns], axis=1
    )


def whole_weight(first, own_ref, other_refs):
    pair = own_ref.shape[0]
    own = jnp.concatenate([own_ref[i] for i in range(pair)], axis=1)
    if not other_refs:
        return own
    other = jnp.concatenate([other_refs[0][i] for i in range(pair)], axis=1)
    for at, ref in enumerate(other_refs[1:], 1):
        here = jnp.concatenate([ref[i] for i in range(pair)], axis=1)
        other = jnp.where(pl.program_id(0) == at, here, other)
    return jnp.concatenate([jnp.where(first, own, other), jnp.where(first, other, own)], axis=0)


def experts_kernel(blocks, sources, counts, width, place_ref, router_ref, *refs):
    x_refs, g_refs, refs = refs[:sources], refs[sources : 2 * sources], refs[2 * sources :]
    (wg0_ref, wu0_ref, wd0_ref), refs = refs[:3], refs[3:]
    wg1_refs, refs = refs[: counts[0]], refs[counts[0] :]
    wu1_refs, refs = refs[: counts[1]], refs[counts[1] :]
    wd1_refs, refs = refs[: counts[2]], refs[counts[2] :]
    keep_ref, send_ref, own_ref, h_ref, dg_ref, du_ref, *refs = refs
    x_ref, grad_ref, gates_ref, din_acc, dgates_acc = refs
    step, steps = pl.program_id(0), pl.num_programs(0)
    pair, _, units = wg0_ref.shape
    first = place_ref[0] == 0
    base = place_ref[1] + step * pair
    rows = x_ref.shape[0] // blocks

    @pl.when(step == 0)
    def _():
        rows_in = whole_of(x_refs)
        x_ref[...] = rows_in
        grad_ref[...] = whole_of(g_refs)
        mask = grad_ref[:, width:].astype(F32)
        logits = jnp.where(mask > 0, nn(rows_in, router_ref[...]), -1e30)
        gates = mask * jnp.exp(logits - jnp.max(logits, axis=1, keepdims=True))
        gates = gates / jnp.sum(gates, axis=1, keepdims=True)
        gates_ref[...] = gates
        own_ref[...] = gates

    rows_in, rows_grad, gates = x_ref[...], grad_ref[:, :width], gates_ref[...]
    w_gate = whole_weight(first, wg0_ref, wg1_refs)
    w_up = whole_weight(first, wu0_ref, wu1_refs)
    w_down = whole_weight(first, wd0_ref, wd1_refs)
    wide = gate_columns(gates, base, pair, units)
    gate_pre, up_pre = nn(rows_in, w_gate), nn(rows_in, w_up)
    sigma = 0.5 * jnp.tanh(0.5 * gate_pre) + 0.5
    silu_gate = gate_pre * sigma
    active = silu_gate * up_pre
    h_ref[...] = (wide * active).astype(BF16)
    raw = nn(rows_grad, w_down)
    product = raw * active
    lane = lax.broadcasted_iota(jnp.int32, gates.shape, 1)
    d_gates = jnp.zeros_like(gates)
    for i in range(pair):
        column = RESID_MULT * jnp.sum(product[:, i * units : (i + 1) * units], axis=1, keepdims=True)
        d_gates = jnp.where(lane == base + i, column, d_gates)
    d_active = (RESID_MULT * wide) * raw
    d_gate_pre = (d_active * up_pre * sigma * (1.0 + gate_pre * (1.0 - sigma))).astype(BF16)
    d_up_pre = (d_active * silu_gate).astype(BF16)
    dg_ref[...], du_ref[...] = d_gate_pre, d_up_pre
    d_in = nt(d_gate_pre, w_gate) + nt(d_up_pre, w_up)

    @pl.when(step == 0)
    def _():
        din_acc[...] = d_in
        dgates_acc[...] = d_gates

    @pl.when(step > 0)
    def _():
        din_acc[...] += d_in
        dgates_acc[...] += d_gates

    @pl.when(step == steps - 1)
    def _():
        for m in range(blocks):
            ref = (keep_ref, send_ref)[m % 2]
            to, at = slice(m // 2 * rows, (m // 2 + 1) * rows), slice(m * rows, (m + 1) * rows)
            ref[to, :width] = din_acc[at].astype(BF16)
            ref[to, width:] = split_lanes(dgates_acc[at])


def held(a):
    return pl.BlockSpec(a.shape, lambda i: (0,) * len(a.shape))


def run_experts(blocks, chunks, x_blocks, g_blocks, router, place, weights, others):
    tokens, lanes = sum(b.shape[0] for b in x_blocks), g_blocks[0].shape[1]
    width = x_blocks[0].shape[1]
    count, _, units = weights[0].shape
    pair = count // chunks
    moving = lambda w: pl.BlockSpec((pair, w.shape[1], units), lambda i: (i, 0, 0))
    column = pl.BlockSpec((tokens, pair * units), lambda i: (0, i))
    outs = (
        [shape((tokens // 2, lanes), BF16)] * 2
        + [shape((tokens, LANES), F32)]
        + [shape((tokens, count * units), BF16)] * 3
    )
    flat = sum(others, [])
    return pl.pallas_call(
        functools.partial(experts_kernel, blocks, len(x_blocks), [len(o) for o in others], width),
        grid=(chunks,),
        out_shape=tuple(outs),
        in_specs=[pl.BlockSpec(memory_space=pltpu.SMEM), held(router)]
        + [held(b) for b in x_blocks + g_blocks]
        + [moving(w) for w in weights]
        + [held(o) for o in flat],
        out_specs=tuple(held(o) for o in outs[:3]) + (column,) * 3,
        scratch_shapes=[
            pltpu.VMEM((tokens, width), BF16),
            pltpu.VMEM((tokens, lanes), BF16),
            pltpu.VMEM((tokens, LANES), F32),
            pltpu.VMEM((tokens, width), F32),
            pltpu.VMEM((tokens, LANES), F32),
        ],
        compiler_params=pltpu.CompilerParams(vmem_limit_bytes=VMEM_BYTES),
        cost_estimate=cost("experts"),
        name="experts",
    )(place, router, *x_blocks, *g_blocks, *weights, *flat)


def grads_kernel(sources, parts, width, place_ref, *refs):
    x_refs, g_refs, refs = refs[:sources], refs[sources : 2 * sources], refs[2 * sources :]
    h_refs, dg_refs, du_refs = (refs[i * parts : (i + 1) * parts] for i in range(3))
    grad_refs = refs[3 * parts :]
    pair, half, units = grad_refs[0].shape
    first = place_ref[0] == 0

    def halves(grad, own_ref, other_ref):
        own = jnp.where(first, grad[:half], grad[half:]).astype(BF16)
        other = jnp.where(first, grad[half:], grad[:half]).astype(BF16)
        for i in range(pair):
            own_ref[i] = own[:, i * units : (i + 1) * units]
            other_ref[i] = other[:, i * units : (i + 1) * units]

    rows_in, rows_grad = whole_of(x_refs), whole_of(g_refs)[:, :width]
    halves(RESID_MULT * tn(rows_grad, whole_of(h_refs)), grad_refs[4], grad_refs[5])
    halves(tn(rows_in, whole_of(dg_refs)), grad_refs[0], grad_refs[1])
    halves(tn(rows_in, whole_of(du_refs)), grad_refs[2], grad_refs[3])


def run_grads(x_blocks, g_blocks, place, hidden, d_gate, d_up, dims, chunks):
    parts, tokens = len(hidden), sum(b.shape[0] for b in x_blocks)
    count, half, units = dims
    pair = count // chunks
    width = x_blocks[0].shape[1]
    moving = pl.BlockSpec((pair, half, units), lambda i: (i, 0, 0))
    column = pl.BlockSpec((tokens // parts, pair * units), lambda i: (0, i))
    return pl.pallas_call(
        functools.partial(grads_kernel, len(x_blocks), parts, width),
        grid=(chunks,),
        out_shape=(shape(dims, BF16),) * 6,
        in_specs=[pl.BlockSpec(memory_space=pltpu.SMEM)]
        + [held(b) for b in x_blocks + g_blocks]
        + [column] * (3 * parts),
        out_specs=(moving,) * 6,
        compiler_params=pltpu.CompilerParams(vmem_limit_bytes=VMEM_BYTES),
        cost_estimate=cost("grads"),
        name="grads",
    )(place, *x_blocks, *g_blocks, *hidden, *d_gate, *d_up)


def outputs_kernel(blocks, parts, chunks, place_ref, wd0_ref, *refs):
    h_refs, refs = refs[:parts], refs[parts:]
    wd1_refs, out_refs, out_acc = refs[:chunks], refs[chunks:-1], refs[-1]
    step, steps = pl.program_id(0), pl.num_programs(0)
    out = nt(whole_of(h_refs), whole_weight(place_ref[0] == 0, wd0_ref, wd1_refs))

    @pl.when(step == 0)
    def _():
        out_acc[...] = out

    @pl.when(step > 0)
    def _():
        out_acc[...] += out

    @pl.when(step == steps - 1)
    def _():
        rows = out_acc.shape[0] // blocks
        for m in range(blocks):
            out_refs[m % 2 * parts + m // 2][...] = out_acc[m * rows : (m + 1) * rows].astype(BF16)


def run_outputs(place, hidden, w_own, others):
    parts, chunks = len(hidden), len(others)
    count, half, units = w_own.shape
    pair, tokens, width = count // chunks, parts * hidden[0].shape[0], 2 * half
    outs = (shape((tokens // parts // 2, width), BF16),) * (2 * parts)
    column = pl.BlockSpec((tokens // parts, pair * units), lambda i: (0, i))
    return pl.pallas_call(
        functools.partial(outputs_kernel, 2 * parts, parts, chunks),
        grid=(chunks,),
        out_shape=outs,
        in_specs=[
            pl.BlockSpec(memory_space=pltpu.SMEM),
            pl.BlockSpec((pair, half, units), lambda i: (i, 0, 0)),
        ]
        + [column] * parts
        + [held(o) for o in others],
        out_specs=tuple(held(o) for o in outs),
        scratch_shapes=[pltpu.VMEM((tokens, width), F32)],
        compiler_params=pltpu.CompilerParams(vmem_limit_bytes=VMEM_BYTES),
        cost_estimate=cost("outputs"),
        name="outputs",
    )(place, w_own, *hidden, *others)


def rms_back(rows, gain, grad):
    scale = lax.rsqrt(jnp.mean(rows * rows, axis=-1, keepdims=True) + NORM_EPS)
    d_gain = jnp.sum(grad * rows * scale, axis=0, keepdims=True)
    pulled = grad * gain
    mean = jnp.mean(pulled * rows, axis=-1, keepdims=True)
    return scale * pulled - rows * (scale * scale * scale) * mean, d_gain


def body(
    hidden_in,
    positions,
    routes,
    out_grad,
    attn_gain,
    query_weight,
    key_matrix,
    value_matrix,
    out_weight,
    moe_gain,
    router_weight,
    gate_weight,
    up_weight,
    down_weight,
):
    shards, contexts, tensors = (lax.axis_size(a) for a in ("shards", "context", "tensor"))
    shard, context, tensor = (lax.axis_index(a) for a in ("shards", "context", "tensor"))
    owners = shards * contexts
    steps = stepped()
    owner = shard * contexts + context if steps else 0 * shard
    flip = context if steps else 0 * context
    rows, width = hidden_in.shape[1:]
    chunk, quarter = width // owners, rows // tensors
    wide, narrow = query_weight.shape[1], key_matrix.shape[1]
    heads, group = wide // HEAD_SIZE, wide // narrow
    expert_count, local_experts = router_weight.shape[1], gate_weight.shape[0]
    columns = 2 * wide + 2 * narrow
    gates_at = tensor if steps else context * tensors + tensor
    place = jnp.stack([shard, context * local_experts, flip, owner, tensor, gates_at])
    place = place.astype(jnp.int32)

    packed = jnp.concatenate(
        [
            jnp.concatenate([query_weight, key_matrix, value_matrix, out_weight], axis=1),
            jnp.pad(
                jnp.concatenate([attn_gain, moe_gain])[None], ((0, 7), (0, columns - 2 * chunk))
            ),
            jnp.pad(
                router_weight.reshape(8, chunk * expert_count // 8),
                ((0, 0), (0, columns - chunk * expert_count // 8)),
            ),
        ],
        axis=0,
    )
    grad_rows = out_grad[0]
    names = jnp.arange(LANES, dtype=jnp.int32)
    mask = jnp.any(routes[0][:, :, None] == names[None, None, :], axis=1).astype(BF16)
    gathered = gather_owners(packed)
    if steps:
        even, odd = gathered[:4], gathered[4:]
        pieces = [p for pair in zip(even, odd) for p in pair]
        gain_a = jnp.concatenate([p[chunk : chunk + 1, :chunk] for p in pieces], axis=1).astype(F32)
    else:
        stack = gathered[0]
        pieces = [stack[:, :chunk].reshape(width, columns)]
        gain_a = stack[:, chunk, :chunk].reshape(1, width).astype(F32)

    chunks = 2 if local_experts % 2 == 0 else 1
    size = local_experts // chunks
    weights = [lax.all_gather(w, "shards", axis=1, tiled=True) for w in (gate_weight, up_weight)]
    weights.append(down_weight)
    down_other = [swap(down_weight[i * size : (i + 1) * size], "shards", 1) for i in range(chunks)]
    others = [[], [], down_other]

    place_all = positions[0].reshape(contexts, rows)
    own_places = cut(place_all, context, 1).reshape(rows, 1)
    if steps:
        place_all = jnp.concatenate(xor_blocks([place_all[i] for i in range(contexts)], context))
    all_places = place_all.reshape(1, contexts * rows)
    half = HEAD_SIZE // 2
    frequency = ROPE_BASE ** (-2.0 * jnp.arange(half, dtype=F32) / HEAD_SIZE)
    angles = own_places.astype(F32) * frequency[None, :]
    cosine, sine = jnp.cos(angles), jnp.sin(angles)
    cosine = jnp.concatenate([cosine] * 4, axis=1)
    sine = jnp.concatenate([-sine, sine] * 2, axis=1)

    hidden = hidden_in[0]
    hidden_rel = hidden
    if steps:
        hidden_rel = jnp.concatenate(xor_blocks(columns_of(hidden, owners), owner), axis=1)
    normed_a, query, kv, w_qkv = project(
        hidden_rel, gain_a, pieces, cosine, sine, wide, narrow, chunk if steps else width
    )
    kv_all = gather_context(kv)
    attended, lse = attend(query, kv_all, own_places, all_places, heads, group)

    if steps:
        evens = jnp.concatenate([p[:chunk, columns - wide :] for p in even], axis=0)
        bit = 1
        while bit < tensors:
            evens = jnp.concatenate([evens, after(swap(evens, "tensor", bit), query)], axis=0)
            bit *= 2
        w_out = call(
            functools.partial(assemble_kernel, (0, 2, 4, 6, 1, 3, 5, 7), chunk),
            [shape((width, wide * tensors), BF16)],
            (evens, swap(after(evens, attended), "context", 1)),
            "assemble",
            smem=(place,),
        )[0]
        late = [after(p, query) for p in pieces]
        gain_m = [p[chunk : chunk + 1, chunk : 2 * chunk] for p in late]
        gain_m = jnp.concatenate(xor_blocks(gain_m, owner), axis=1).astype(F32)
        router = [p[chunk + 8 : chunk + 16, : chunk * expert_count // 8] for p in late]
        router = jnp.concatenate(xor_blocks(router, owner), axis=0).reshape(width, expert_count)
    else:
        own = pieces[0][:, columns - wide :]
        w_out = jnp.concatenate([own] + [turn(own, k) for k in range(1, tensors)], axis=1)
        gain_m = stack[:, chunk, chunk : 2 * chunk].reshape(1, width).astype(F32)
        router = stack[:, chunk + 8 :, : chunk * expert_count // 8].reshape(width, expert_count)
    router = jnp.pad(router, ((0, 0), (0, LANES - expert_count)))
    attended_all = [attended] + [turn(attended, k) for k in range(1, tensors)]
    middle, normed_m = call(
        middle_kernel,
        (shape(hidden.shape, F32), shape(hidden.shape, BF16)),
        (after(hidden, router, down_other[0]), gain_m, w_out, *attended_all),
        "middle",
    )

    if steps:
        across = swap(normed_m, "context", 2)
        x_blocks = [normed_m, swap(normed_m, "context", 1)]
    else:
        x_blocks = gather_context(normed_m)
    g_blocks = gather_context(jnp.concatenate([grad_rows, mask], axis=1))
    run = lambda xs, gs: run_experts(2, chunks, xs, gs, router, place, weights, others)
    if steps:
        found = [run(x_blocks, g_blocks[:2])]
        across = after(across, found[0][0])
        x_blocks += [across, swap(across, "context", 1)]
        found.append(run(x_blocks[2:], g_blocks[2:]))
    else:
        parts = [
            ([cut(x_blocks[0], i, PART_ROWS)], [cut(g_blocks[0], i, PART_ROWS)])
            for i in range(contexts * rows // PART_ROWS)
        ]
        found = [run(xs, gs) for xs, gs in parts]
    gates = found[0][2] if steps else jnp.concatenate([f[2] for f in found], axis=0)

    def to_quarters(kept, sent, form):
        if steps:
            core = [swap(b, "context", 1) for b in sent]
            send = fold((kept[1], core[1]), place, width, 0)[0]
            return send, fold((kept[0], core[0], swap(send, "context", 2)), place, width, form)
        whole = jnp.concatenate([b for pair in zip(kept, sent) for b in pair], axis=0)
        own = lax.psum_scatter(whole, "context", scatter_dimension=0, tiled=True)
        return own, fold((own,), place, width, form)

    early, d_normed = to_quarters([f[0] for f in found], [f[1] for f in found], tensors)
    hidden_parts = [[f[3] for f in found]] if steps else [[f[3]] for f in found]
    hidden_parts = [[after(h[0], d_normed[0])] + h[1:] for h in hidden_parts]
    outputs = [run_outputs(place, h, down_weight, down_other) for h in hidden_parts]
    if steps:
        outputs = [(outputs[0][i], outputs[0][2 + i]) for i in range(2)]
    dims = gate_weight.shape
    if steps:
        columns_in = [[f[i] for f in found] for i in (3, 4, 5)]
        columns_in[0][0] = after(columns_in[0][0], early)
        grads = run_grads(x_blocks, g_blocks, place, *columns_in, dims, chunks)
    else:
        grads = [
            run_grads(xs, gs, place, [f[3]], [f[4]], [f[5]], dims, chunks)
            for f, (xs, gs) in zip(found, parts)
        ]
        grads = [sum(g.astype(F32) for g in one).astype(BF16) for one in zip(*grads)]

    parts = [d_normed[0]] + [turn(d_normed[k], k) for k in range(1, tensors)]
    outs = (
        shape((quarter, width), F32),
        shape((quarter, width), BF16),
        shape((1, width), F32),
        shape((width, LANES), F32),
        shape((quarter, wide), BF16),
    ) + (shape((quarter, wide + width), BF16),) * (tensors - 1)
    own = lambda lanes: pl.BlockSpec((quarter, lanes), lambda i, at: (at[4], 0))
    gates_own = pl.BlockSpec((quarter, LANES), lambda i, at: (at[5], 0))
    full = lambda a: pl.BlockSpec(a.shape, lambda i, at: (0, 0))
    d_middle, d_attn, d_gain_m, d_router, *d_attended = pl.pallas_call(
        functools.partial(middle_back_kernel, width),
        out_shape=outs,
        grid_spec=pltpu.PrefetchScalarGridSpec(
            num_scalar_prefetch=1,
            grid=(1,),
            in_specs=[own(width), own(width), full(gain_m), own(width), gates_own, full(router), full(w_out)]
            + [full(p) for p in parts],
            out_specs=tuple(full(o) for o in outs),
        ),
        compiler_params=pltpu.CompilerParams(vmem_limit_bytes=VMEM_BYTES),
        cost_estimate=cost("middle_back"),
        name="middle_back",
    )(place, middle, normed_m, gain_m, grad_rows, after(gates, outputs[0][0], grads[0]), router, w_out, *parts)

    came = [swap(grads[i], "shards", 1) for i in (5, 1, 3)]

    d_attended = [turn(d, k) if k else d for k, d in enumerate(d_attended)]
    out_early, moe_out = to_quarters(
        *([after(o[i], d_middle) for o in outputs] for i in range(2)), 0
    )
    d_query, d_kv, d_kv_send = attend_back(
        contexts if steps else 2,
        after(query, came[0], out_early),
        kv_all,
        own_places,
        all_places,
        lse,
        d_attended,
        place,
        cosine,
        sine,
        heads,
        group,
    )
    exchange = lambda x: lax.all_to_all(x, "tensor", 0, 0, tiled=True)
    moe_rows = exchange(moe_out[0].reshape(tensors, quarter, width))
    moe_rows = jnp.sum(moe_rows.astype(F32), axis=0)
    block_out = (cut(middle, tensor, quarter) + RESID_MULT * moe_rows).astype(BF16)
    if steps:
        d_kv = d_kv.astype(F32) + swap(d_kv_send, "context", 1).astype(F32)
        d_kv, d_kv_send = d_kv[:rows], swap(d_kv[rows:].astype(BF16), "context", 2)
    else:
        d_kv = jnp.concatenate([d_kv, d_kv_send], axis=0)
        d_kv = lax.psum_scatter(d_kv, "context", scatter_dimension=0, tiled=True)
        d_kv_send = jnp.zeros_like(d_kv)
    *d_normed, d_lin, d_gain_a = call(
        functools.partial(project_back_kernel, narrow),
        [shape((quarter, width), F32)]
        + [shape((quarter, width), BF16)] * (tensors - 1)
        + [shape((rows, wide + 2 * narrow), BF16), shape((1, width), F32)],
        (after(d_query, came[1], moe_out[0]), d_kv, d_kv_send, cosine[:, :narrow], sine[:, :narrow], w_qkv, hidden_rel),
        "project_back",
        smem=(place,),
        scratch_shapes=[pltpu.VMEM((rows, width), F32)],
    )
    parts = [turn(d_normed[k], k) for k in range(1, tensors)]
    if steps:
        kept, sent = call(
            functools.partial(weights_back_kernel, OWNER_ORDER, chunk),
            [shape((width // 2, columns), BF16)] * 2,
            (normed_a, after(d_lin, parts[0]), attended, d_attn, *d_attended[1:]),
            "weights_back",
            smem=(place,),
            scratch_shapes=[pltpu.VMEM((rows, width), BF16), pltpu.VMEM((width, wide), F32)],
        )
        tie, d_weights = scatter_owners(kept, sent, BF16)
    d_normed = d_normed[0] + sum(p.astype(F32) for p in parts)
    d_rows, _unused = rms_back(
        cut(hidden_rel, tensor, quarter).astype(F32), gain_a, d_normed
    )
    if steps:
        d_rows = jnp.concatenate(xor_blocks(columns_of(d_rows, owners), owner), axis=1)
    both = jnp.concatenate([(d_middle + d_rows).astype(BF16), block_out], axis=1)
    late = both
    both = gather_tensor(both)
    in_grad, block_out = both[:, :width].astype(F32), both[:, width:]

    expert_grads = [
        after(own, late).astype(F32) + other.astype(F32)
        for own, other in ((grads[0], came[1]), (grads[2], came[2]), (grads[4], came[0]))
    ]
    small = jnp.concatenate([d_gain_m, d_router[:, :expert_count].T], axis=0)
    d_gain_a = after(d_gain_a, late)
    if steps:
        small = xor_blocks(columns_of(small, owners), owner)
        small = [
            jnp.concatenate([a, b], axis=0) for a, b in zip(columns_of(d_gain_a, owners), small)
        ]
        small = [jnp.pad(b, ((0, -b.shape[0] % 8), (0, 0))) for b in small]
        kept, sent = (
            jnp.concatenate([small[r] for r in OWNER_ORDER[i : i + 4]], axis=0) for i in (0, 4)
        )
        small = scatter_owners(kept, sent, F32)[1]
    else:
        over = ("shards", "context")
        attn_rows = [d_attn] + [d[:, wide:] for d in d_attended[1:]]
        attn_rows = jnp.concatenate(xor_blocks(attn_rows, tensor), axis=0)
        d_weights = jnp.concatenate([tn(normed_a, d_lin), tn(attn_rows, attended)], axis=1)
        d_weights = lax.psum_scatter(
            d_weights.astype(BF16), over, scatter_dimension=0, tiled=True
        ).astype(F32)
        small = jnp.concatenate([d_gain_a, small], axis=0)
        small = jnp.swapaxes(small.reshape(-1, owners, chunk), 0, 1)
        small = lax.psum_scatter(small, over, scatter_dimension=0)
    small = butterfly(small)
    return (
        block_out[None],
        in_grad[None],
        small[0],
        d_weights[:, :wide],
        d_weights[:, wide : wide + narrow],
        d_weights[:, wide + narrow : wide + 2 * narrow],
        d_weights[:, wide + 2 * narrow :],
        small[1],
        small[2 : 2 + expert_count].T,
        expert_grads[0],
        expert_grads[1],
        expert_grads[2],
    )


def solution(mesh):
    owned = ("shards", "context")
    rows = P("shards", "context", None)
    split = P(owned, "tensor")
    expert = P("context", "shards", "tensor")
    return jax.shard_map(
        body,
        mesh=mesh,
        in_specs=(
            rows,
            P("shards", None),
            rows,
            rows,
            P(owned),
            split,
            split,
            split,
            split,
            P(owned),
            P(owned, None),
            expert,
            expert,
            expert,
        ),
        out_specs=(
            rows,
            rows,
            P(owned),
            split,
            split,
            split,
            split,
            P(owned),
            P(owned, None),
            expert,
            expert,
            expert,
        ),
        check_vma=False,
    )
```
